256 devices in a mesh: dp: 2 (over core), expert: 8 (over z), tensor: 16 (over y, x).
Axes of the slice: x: 4, y: 4, z: 8, core: 2. Of those that a mesh axis runs over, the one named last changes fastest.
Arguments:
- tokens: bfloat16 [2048, 3072], P(('dp', 'expert', 'tensor')), may hold values from -6 to 6
- expert_ids: int32 [2048, 2], P(('dp', 'expert', 'tensor')), may hold values from 0 to 7, all different within a row; in each aligned block of 8 rows (0 to 7, 8 to 15, ...) at most 4 rows name the same one
- gate_values: bfloat16 [2048, 2], P(('dp', 'expert', 'tensor')), may hold values from 0.099609375 to 1
- cotangent: bfloat16 [2048, 3072], P(('dp', 'expert', 'tensor')), may hold values from -6 to 6
- w_gate: bfloat16 [8, 3072, 8192], P('expert', None, ('dp', 'tensor')), may hold values from -0.109375 to 0.109375
- w_up: bfloat16 [8, 3072, 8192], P('expert', None, ('dp', 'tensor')), may hold values from -0.109375 to 0.109375
- w_down: bfloat16 [8, 8192, 3072], P('expert', ('dp', 'tensor')), may hold values from -0.0625 to 0.0625
Outputs:
- moe_out: bfloat16 [2048, 3072], P(('dp', 'expert', 'tensor'))
- d_tokens: bfloat16 [2048, 3072], P(('dp', 'expert', 'tensor'))
- d_w_gate: bfloat16 [8, 3072, 8192], P('expert', None, ('dp', 'tensor'))
- d_w_up: bfloat16 [8, 3072, 8192], P('expert', None, ('dp', 'tensor'))
- d_w_down: bfloat16 [8, 8192, 3072], P('expert', ('dp', 'tensor'))
The draws below stay inside these ranges and needn't reach their ends.
Inputs may be any that keep to these rules, and one draw needn't show every extreme that they name: `expert_ids`: within the rows of one device (8 tokens) each expert is named at most 4 times, a bound that some block reaches; the 2 ids of a token differ.
All inputs are finite; a program needn't handle non-finite values.
Results may differ from the reference program's by a relative error of at most 0.02.
Values may be sent and summed in bfloat16 or wider, within the bound.
No kernel may reach another device: no remote copies, remote signals or barrier semaphores. Data moves between devices by JAX's collectives and lax.ppermute only.
A program may use at most 128 MiB of HBM per device.

```python
import math
import jax
import jax.numpy as jnp
import numpy as np
from jax import lax

D = 3072
FF = 8192
TOP = 2
TOK_DEV = 8
EXPERTS = 8
REPLICAS = 2
MOST = 4
TOKENS = 2048
N_DP = 2
N_TENSOR = 16


def levels(key, dims, shards, low, top_value):
    def one(position, blocks):
        heights = jax.random.uniform(jax.random.fold_in(jax.random.fold_in(key, 6), position), (blocks,), jnp.float32, low / len(shards), top_value / len(shards))
        return jnp.repeat(jnp.exp(heights), dims[position] // blocks).reshape((-1,) + (1,) * (len(dims) - position - 1))

    gain = one(*shards[0])
    for cut in shards[1:]:
        gain = gain * one(*cut)
    return gain


def shared_out(stream_key, own, number, rows, count, top, most, slope):
    ranking = jax.random.permutation(stream_key, count)
    crowded, ordinary = load_shares(count, rows * top, most, slope, True), load_shares(count, rows * top, most, slope, False)
    places = jnp.arange(count)

    def named(tallies, offset_by):
        used = int((tallies > 0).sum())
        fixed = max(1, used // 4)
        moved = fixed + (places - fixed + offset_by * (used - fixed)) % max(1, count - fixed)
        return jnp.zeros((count,), jnp.int32).at[ranking[jnp.where(places < fixed, places, moved)]].set(jnp.asarray(tallies, jnp.int32))

    tallies = jnp.where(number % 4 == 0, named(crowded, number // 4), named(ordinary, number - number // 4 - 1))
    mixed = jax.random.permutation(jax.random.fold_in(own, 3), count)
    giver, sink = mixed[0:count // 2 * 2:2], mixed[1:count // 2 * 2:2]
    margin = jnp.minimum(tallies[giver] - 1, most - tallies[sink]) // 2
    margin = jnp.where((giver == ranking[0]) | (sink == ranking[0]) | (tallies[sink] == 0), 0, jnp.maximum(margin, 0))
    moved = jax.random.randint(jax.random.fold_in(own, 4), (count // 2,), 0, 1 << 20) % (margin + 1)
    tallies = tallies.at[giver].add(-moved).at[sink].add(moved)
    items = jnp.searchsorted(jnp.cumsum(tallies), jnp.arange(rows * top), side="right").astype(jnp.int32)
    listing = items.reshape(top, rows).T
    listing = listing[jax.random.permutation(jax.random.fold_in(own, 1), rows)]
    offset_by = jax.random.randint(jax.random.fold_in(own, 2), (rows, 1), 0, top)
    return jnp.take_along_axis(listing, (jnp.arange(top)[None, :] + offset_by) % top, axis=1)


def load_shares(count, total, reach, lean, full):
    portions = [(1 << 20) // math.isqrt(standing ** lean) + 1 for standing in range(1, count + 1)]
    largest = reach if full else min(reach, max(-(-total // count), total * portions[0] // sum(portions)))
    least = 1 if total - largest >= count - 1 else 0
    holding, spare = [largest] + [least] * (count - 1), total - largest - least * (count - 1)
    while spare > 0:
        movable = [i for i in range(1, count) if holding[i] < largest] or [i for i in range(1, count) if holding[i] < reach]
        whole, left = sum([portions[i] for i in movable]), spare
        for i in movable:
            more = min(reach - holding[i], max(1, left * portions[i] // whole), spare)
            holding[i] = holding[i] + more
            spare = spare - more
    return np.array(holding)


def bell_draw(rng, extent, scale, reach, shards=(), kind=jnp.bfloat16):
    drawn = jax.random.normal(rng, extent, jnp.float32) * scale
    if len(shards) > 0:
        drawn = levels(rng, extent, shards, -0.22, 0.18) * drawn
    return jnp.clip(drawn, min=-reach, max=reach).astype(kind)


def setup_inputs(seed: int = 0) -> dict:
    seeds = jax.random.split(jax.random.key(seed), 8)
    tokens = bell_draw(seeds[0], (TOKENS, D), 1.0, 6.0, ((0, 256),))
    expert_ids_keys = jax.random.split(jax.random.fold_in(seeds[1], 1), TOKENS // TOK_DEV)
    expert_ids_turns = jax.random.permutation(jax.random.fold_in(seeds[1], 3), TOKENS // TOK_DEV)
    expert_ids = jax.vmap(lambda own, number: shared_out(jax.random.fold_in(seeds[1], 2), own, number, TOK_DEV, EXPERTS, TOP, MOST, 1))(expert_ids_keys, expert_ids_turns).reshape((TOKENS, TOP))
    gate_values = jnp.clip(jnp.exp(math.log(1.0) - 2.306499 * jax.random.uniform(seeds[2], (TOKENS, TOP), jnp.float32) ** levels(seeds[2], (TOKENS, TOP), ((0, 256),), -0.2, 0.2)), 0.099609375, 1.0).astype(jnp.bfloat16)
    cotangent = bell_draw(seeds[3], (TOKENS, D), 1.0, 6.0, ((0, 256),))
    w_gate = bell_draw(seeds[4], (EXPERTS, D, FF), D ** -0.5, 0.109375, ((0, 8), (2, 32)))
    w_up = bell_draw(seeds[5], (EXPERTS, D, FF), D ** -0.5, 0.109375, ((0, 8), (2, 32)))
    w_down = bell_draw(seeds[6], (EXPERTS, FF, D), FF ** -0.5, 0.0625, ((0, 8), (1, 32)))
    return dict(tokens=tokens, expert_ids=expert_ids, gate_values=gate_values, cotangent=cotangent, w_gate=w_gate, w_up=w_up, w_down=w_down)


def contract_last(left, right):
    return lax.dot_general(left, right, (((1,), (1,)), ((), ())), preferred_element_type=jnp.float32)


def contract_first(left, right):
    return lax.dot_general(left, right, (((0,), (0,)), ((), ())), preferred_element_type=jnp.float32)


def to_bf16_f32(value):
    rounded = lax.optimization_barrier(value.astype(jnp.bfloat16))
    return rounded.astype(jnp.float32)


def expert_pass(rows_x, rows_dy, gate_mat, up_mat, down_mat):
    block_width = FF // (N_DP * N_TENSOR)
    row_total = rows_x.shape[0]
    gate_proj = jnp.dot(rows_x, gate_mat, preferred_element_type=jnp.float32)
    up_proj = jnp.dot(rows_x, up_mat, preferred_element_type=jnp.float32)
    sigmoid_gate = jax.nn.sigmoid(gate_proj)
    activated = gate_proj * sigmoid_gate
    hidden = (activated * up_proj).astype(jnp.bfloat16)
    hidden_grad = contract_last(rows_dy, down_mat)
    gate_grad = (hidden_grad * up_proj * sigmoid_gate * (1.0 + gate_proj * (1.0 - sigmoid_gate))).astype(jnp.bfloat16)
    up_grad = (hidden_grad * activated).astype(jnp.bfloat16)
    hidden_four = hidden.reshape(row_total, N_DP, N_TENSOR, block_width)
    ggrad_four = gate_grad.reshape(row_total, N_DP, N_TENSOR, block_width)
    ugrad_four = up_grad.reshape(row_total, N_DP, N_TENSOR, block_width)
    down_four = down_mat.reshape(N_DP, N_TENSOR, block_width, D)
    gmat_four = gate_mat.reshape(D, N_DP, N_TENSOR, block_width)
    umat_four = up_mat.reshape(D, N_DP, N_TENSOR, block_width)
    out_total = jnp.zeros((row_total, D), jnp.float32)
    back_total = jnp.zeros((row_total, D), jnp.float32)
    for group in range(N_TENSOR):
        out_group = jnp.zeros((row_total, D), jnp.float32)
        back_group = jnp.zeros((row_total, D), jnp.float32)
        for replica in range(N_DP):
            out_group = out_group + jnp.dot(hidden_four[:, replica, group], down_four[replica, group],
                                            preferred_element_type=jnp.float32)
            back_group = back_group + contract_last(ggrad_four[:, replica, group], gmat_four[:, replica, group])
            back_group = back_group + contract_last(ugrad_four[:, replica, group], umat_four[:, replica, group])
        out_total = out_total + to_bf16_f32(out_group)
        back_total = back_total + to_bf16_f32(back_group)
    result = out_total.astype(jnp.bfloat16)
    row_back = back_total.astype(jnp.bfloat16)
    grad_gate = contract_first(rows_x, gate_grad)
    grad_up = contract_first(rows_x, up_grad)
    grad_down = contract_first(hidden, rows_dy)
    return result, row_back, grad_gate, grad_up, grad_down


def reference(tokens, expert_ids, gate_values, cotangent, w_gate, w_up, w_down):
    half_rows = TOKENS // REPLICAS
    capacity = (half_rows // TOK_DEV) * MOST
    entry_count = half_rows * TOP
    order = jnp.arange(entry_count, dtype=jnp.int32)

    def per_expert(carry, inputs):
        out_total, back_total = carry
        expert, gate_mat, up_mat, down_mat = inputs
        sum_gate = jnp.zeros((D, FF), jnp.float32)
        sum_up = jnp.zeros((D, FF), jnp.float32)
        sum_down = jnp.zeros((FF, D), jnp.float32)
        for replica in range(REPLICAS):
            start = replica * half_rows
            x_part = tokens[start:start + half_rows]
            cot_part = cotangent[start:start + half_rows]
            flat_ids = expert_ids[start:start + half_rows].reshape(-1)
            flat_gate = gate_values[start:start + half_rows].reshape(-1).astype(jnp.float32)
            sort_keys = jnp.where(flat_ids == expert, order, entry_count)
            picked = jnp.sort(sort_keys)[:capacity]
            is_valid = picked < entry_count
            safe_index = jnp.where(is_valid, picked, 0).astype(jnp.int32)
            token_index = (safe_index // TOP).astype(jnp.int32)
            gate_weight = jnp.where(is_valid, flat_gate[safe_index], jnp.float32(0.0))
            rows_x = jnp.where(is_valid[:, None], x_part[token_index], jnp.zeros((), jnp.bfloat16)).astype(jnp.bfloat16)
            rows_dy = (gate_weight[:, None] * cot_part[token_index].astype(jnp.float32)).astype(jnp.bfloat16)
            result, row_back, grad_gate, grad_up, grad_down = expert_pass(rows_x, rows_dy, gate_mat, up_mat, down_mat)
            contrib = gate_weight[:, None] * result.astype(jnp.float32)
            back_rows = jnp.where(is_valid[:, None], row_back.astype(jnp.float32), jnp.float32(0.0))
            out_total = out_total.at[start + token_index].add(contrib)
            back_total = back_total.at[start + token_index].add(back_rows)
            sum_gate = sum_gate + to_bf16_f32(grad_gate)
            sum_up = sum_up + to_bf16_f32(grad_up)
            sum_down = sum_down + to_bf16_f32(grad_down)
        grads = (sum_gate.astype(jnp.bfloat16), sum_up.astype(jnp.bfloat16), sum_down.astype(jnp.bfloat16))
        return (out_total, back_total), grads

    start_carry = (jnp.zeros((TOKENS, D), jnp.float32), jnp.zeros((TOKENS, D), jnp.float32))
    expert_list = jnp.arange(EXPERTS, dtype=jnp.int32)
    (out_total, back_total), (d_w_gate, d_w_up, d_w_down) = lax.scan(
        per_expert, start_carry, (expert_list, w_gate, w_up, w_down))
    return (out_total.astype(jnp.bfloat16), back_total.astype(jnp.bfloat16), d_w_gate, d_w_up, d_w_down)
```

```python
import jax
import jax.numpy as jnp
from jax import lax
from jax.sharding import PartitionSpec as P

BF16 = jnp.bfloat16
F32 = jnp.float32
SIDE = 4


def matmul(left, right, left_dim=1, right_dim=0):
    return lax.dot_general(
        left, right, (((left_dim,), (right_dim,)), ((), ())), preferred_element_type=F32
    )


def shift_x(block, step):
    pairs = [
        (y * SIDE + x, y * SIDE + (x + step) % SIDE) for y in range(SIDE) for x in range(SIDE)
    ]
    return lax.ppermute(block, "tensor", pairs)


def shift_y(block, step):
    pairs = [
        (y * SIDE + x, (y + step) % SIDE * SIDE + x) for y in range(SIDE) for x in range(SIDE)
    ]
    return lax.ppermute(block, "tensor", pairs)


def swap_dp(block):
    return lax.ppermute(block, "dp", [(0, 1), (1, 0)])


def ring_gather(block, shift):
    half = block.shape[0] // 2
    before = shift(block, 1)
    after = shift(block, -1)
    far_low = shift(before[:half], 1)
    far_high = shift(after[half:], -1)
    return [block, before, after, jnp.concatenate([far_low, far_high], axis=0)]


def ring_scatter(parts, shift):
    own, before, after, far = parts
    half = far.shape[0] // 2
    far16 = far.astype(BF16)
    low = shift(far16[:half], -1).astype(F32)
    high = shift(far16[half:], 1).astype(F32)
    before = jnp.concatenate([before[:half] + low, before[half:]], axis=0).astype(BF16)
    after = jnp.concatenate([after[:half], after[half:] + high], axis=0).astype(BF16)
    return own + shift(before, -1).astype(F32) + shift(after, 1).astype(F32)


def swap_order(blocks, rows):
    width = blocks.shape[1]
    return (
        blocks.reshape(SIDE, SIDE, rows, width).transpose(1, 0, 2, 3).reshape(blocks.shape)
    )


def route(expert_ids, gate_values, experts, slots):
    rows, top = expert_ids.shape
    flat = expert_ids.reshape(-1)
    hit = (flat[:, None] == jnp.arange(experts, dtype=jnp.int32)[None, :]).astype(jnp.int32)
    before = jnp.cumsum(hit, axis=0) - hit
    position = jnp.sum(before * hit, axis=1)
    at_slot = position[:, None] == jnp.arange(slots, dtype=jnp.int32)[None, :]
    chosen = (hit.astype(bool)[:, :, None] & at_slot[:, None, :]).astype(F32)
    chosen = chosen.reshape(rows, top, experts, slots)
    select = jnp.sum(chosen, axis=1)
    weighted = jnp.sum(chosen * gate_values.astype(F32)[:, :, None, None], axis=1)
    return (
        jnp.transpose(select, (1, 2, 0)).astype(BF16),
        jnp.transpose(weighted, (1, 2, 0)).astype(BF16),
    )


def body(tokens, expert_ids, gate_values, cotangent, w_gate, w_up, w_down):
    tok_rows, width = tokens.shape
    top = expert_ids.shape[1]
    experts = lax.axis_size("expert")
    slots = max(2, tok_rows * top // experts * 2)
    rows = experts * slots

    gate_mat = jnp.concatenate([w_gate[0], swap_dp(w_gate[0])], axis=1)
    up_mat = jnp.concatenate([w_up[0], swap_dp(w_up[0])], axis=1)
    down_mat = jnp.concatenate([w_down[0], swap_dp(w_down[0])], axis=0)
    own_units = w_gate.shape[2]

    select, weighted = route(expert_ids, gate_values, experts, slots)
    zero = jnp.zeros_like(select)
    spread = jnp.concatenate(
        [
            jnp.concatenate([select, zero], axis=2),
            jnp.concatenate([zero, weighted], axis=2),
        ],
        axis=1,
    ).reshape(2 * rows, 2 * tok_rows)
    both = jnp.concatenate([tokens, cotangent], axis=0)
    send = matmul(spread, both).astype(BF16).reshape(experts, 2 * slots, width)
    recv = lax.all_to_all(send, "expert", split_axis=0, concat_axis=0, tiled=True)
    x_own = recv[:, :slots].reshape(rows, width)
    dy_own = recv[:, slots:].reshape(rows, width)

    x_line = jnp.concatenate(ring_gather(x_own, shift_x), axis=0)
    dy_line = jnp.concatenate(ring_gather(dy_own, shift_y), axis=0)
    x_parts = ring_gather(x_line, shift_y)
    dy_parts = ring_gather(dy_line, shift_x)

    gate_proj = jnp.concatenate([matmul(part, gate_mat) for part in x_parts], axis=0)
    up_proj = jnp.concatenate([matmul(part, up_mat) for part in x_parts], axis=0)
    hidden_grad = swap_order(
        jnp.concatenate([matmul(part, down_mat, 1, 1) for part in dy_parts], axis=0), rows
    )
    sigmoid_gate = jax.nn.sigmoid(gate_proj)
    activated = gate_proj * sigmoid_gate
    hidden = swap_order((activated * up_proj).astype(BF16), rows)
    gate_grad = (
        hidden_grad * up_proj * sigmoid_gate * (1.0 + gate_proj * (1.0 - sigmoid_gate))
    ).astype(BF16)
    up_grad = (hidden_grad * activated).astype(BF16)

    line = SIDE * rows
    out_parts = [matmul(hidden[i * line : (i + 1) * line], down_mat) for i in range(SIDE)]
    back_parts = [
        matmul(gate_grad[i * line : (i + 1) * line], gate_mat, 1, 1)
        + matmul(up_grad[i * line : (i + 1) * line], up_mat, 1, 1)
        for i in range(SIDE)
    ]
    out_line = ring_scatter(out_parts, shift_x)
    back_line = ring_scatter(back_parts, shift_y)
    out_own = ring_scatter([out_line[i * rows : (i + 1) * rows] for i in range(SIDE)], shift_y)
    back_own = ring_scatter([back_line[i * rows : (i + 1) * rows] for i in range(SIDE)], shift_x)

    x_all = jnp.concatenate(x_parts, axis=0)
    dy_all = jnp.concatenate(dy_parts, axis=0)
    grad_gate = matmul(x_all, gate_grad, 0, 0).astype(BF16)
    grad_up = matmul(x_all, up_grad, 0, 0).astype(BF16)
    grad_down = matmul(hidden, dy_all, 0, 0).astype(BF16)
    d_gate = grad_gate[:, :own_units].astype(F32) + swap_dp(grad_gate[:, own_units:]).astype(F32)
    d_up = grad_up[:, :own_units].astype(F32) + swap_dp(grad_up[:, own_units:]).astype(F32)
    d_down = grad_down[:own_units].astype(F32) + swap_dp(grad_down[own_units:]).astype(F32)

    home = jnp.concatenate(
        [
            out_own.astype(BF16).reshape(experts, slots, width),
            back_own.astype(BF16).reshape(experts, slots, width),
        ],
        axis=1,
    )
    home = lax.all_to_all(home, "expert", split_axis=0, concat_axis=0, tiled=True)
    home = home.reshape(2 * rows, width)
    gather = jnp.concatenate(
        [
            jnp.concatenate([weighted, zero], axis=1),
            jnp.concatenate([zero, select], axis=1),
        ],
        axis=2,
    ).reshape(2 * rows, 2 * tok_rows)
    final = matmul(gather, home, 0, 0).astype(BF16)
    return (
        final[:tok_rows],
        final[tok_rows:],
        d_gate.astype(BF16)[None],
        d_up.astype(BF16)[None],
        d_down.astype(BF16)[None],
    )


def solution(mesh):
    token_spec = P(("dp", "expert", "tensor"), None)
    column_spec = P("expert", None, ("dp", "tensor"))
    row_spec = P("expert", ("dp", "tensor"), None)
    in_specs = (token_spec,) * 4 + (column_spec, column_spec, row_spec)
    out_specs = (token_spec, token_spec, column_spec, column_spec, row_spec)
    return jax.shard_map(body, mesh=mesh, in_specs=in_specs, out_specs=out_specs, check_vma=False)
```

```python
import functools

import jax
import jax.numpy as jnp
from jax import lax
from jax.experimental import pallas as pl
from jax.experimental.pallas import tpu as pltpu
from jax.sharding import PartitionSpec as P

BF16 = jnp.bfloat16
F32 = jnp.float32
SIDE = 4
SLOTS = 4
VMEM_LIMIT = 40 * 1024 * 1024
IN_VMEM = pl.BlockSpec(memory_space=pltpu.VMEM)
IN_SMEM = pl.BlockSpec(memory_space=pltpu.SMEM)


def dot(left, right, left_dim=1, right_dim=0):
    return lax.dot_general(
        left, right, (((left_dim,), (right_dim,)), ((), ())), preferred_element_type=F32
    )


def call(kernel, out_shape, flops=0, moved=0):
    def run(*args):
        specs = [IN_SMEM if a.shape == (1,) else IN_VMEM for a in args]
        outs = jax.tree.map(lambda _: IN_VMEM, out_shape)
        return pl.pallas_call(
            kernel,
            out_shape=out_shape,
            in_specs=specs,
            out_specs=outs,
            cost_estimate=pl.CostEstimate(flops=flops, bytes_accessed=moved, transcendentals=0),
            compiler_params=pltpu.CompilerParams(vmem_limit_bytes=VMEM_LIMIT),
        )(*args)

    return run


def shape(*dims):
    return jax.ShapeDtypeStruct(dims, BF16)


def shift(block, step, second):
    pairs = []
    for core in range(2):
        for y in range(SIDE):
            for x in range(SIDE):
                if (core == 0) != second:
                    target = y * SIDE + (x + step) % SIDE
                else:
                    target = (y + step) % SIDE * SIDE + x
                base = core * SIDE * SIDE
                pairs.append((base + y * SIDE + x, base + target))
    return lax.ppermute(block, ("dp", "tensor"), pairs)


def swap(block):
    return lax.ppermute(block, "dp", [(0, 1), (1, 0)])


def exchange(rows, parts):
    blocks = rows.reshape(parts, rows.shape[0] // parts, rows.shape[1])
    moved = lax.all_to_all(blocks, ("dp", "expert"), split_axis=0, concat_axis=0, tiled=True)
    return moved.reshape(rows.shape)


def spread(ids, gates, experts):
    tokens = ids.shape[1]
    dims = (experts * 2 * SLOTS, tokens)
    row = lax.broadcasted_iota(jnp.int32, dims, 0)
    expert, half, slot = row // (2 * SLOTS), row // SLOTS % 2, row % SLOTS
    first, second = ids[0:1, :] == expert, ids[1:2, :] == expert
    named = jnp.where(first | second, 1.0, 0.0).astype(F32)
    earlier = lax.broadcasted_iota(jnp.int32, (tokens, tokens), 0)
    later = lax.broadcasted_iota(jnp.int32, (tokens, tokens), 1)
    place = dot(named, jnp.where(earlier < later, 1.0, 0.0).astype(F32))
    select = jnp.where(place == slot.astype(F32), named, 0.0)
    weight = jnp.where(first, gates[0:1, :], 0.0) + jnp.where(second, gates[1:2, :], 0.0)
    weighted = select * weight
    return (
        [jnp.where(half == h, select, 0.0) for h in range(2)],
        [jnp.where(half == h, weighted, 0.0) for h in range(2)],
    )


def dispatch_kernel(experts, ids_ref, gates_ref, tokens_ref, cotangent_ref, send_ref):
    select, weighted = spread(ids_ref[...], gates_ref[...].astype(F32), experts)
    width = tokens_ref.shape[1] // 2
    rows = experts * 2 * SLOTS
    for mats, ref, start in ((select, tokens_ref, 0), (weighted, cotangent_ref, rows)):
        total = dot(mats[0], ref[:, :width].astype(F32)) + dot(
            mats[1], ref[:, width:].astype(F32)
        )
        send_ref[start : start + rows, :] = total.astype(BF16)


def combine_kernel(experts, ids_ref, gates_ref, home_ref, out_ref, back_ref):
    select, weighted = spread(ids_ref[...], gates_ref[...].astype(F32), experts)
    width = out_ref.shape[1] // 2
    rows = experts * 2 * SLOTS
    for mats, ref, start in ((weighted, out_ref, 0), (select, back_ref, rows)):
        part = home_ref[start : start + rows, :].astype(F32)
        for h in range(2):
            ref[:, h * width : (h + 1) * width] = dot(mats[h], part, 0, 0).astype(BF16)


def half_matrix(rows, half, flip):
    dims = (2 * rows, rows) if flip else (rows, 2 * rows)
    plain = lax.broadcasted_iota(jnp.int32, dims, 1 if flip else 0)
    mixed = lax.broadcasted_iota(jnp.int32, dims, 0 if flip else 1)
    same = (mixed // (2 * SLOTS) == plain // SLOTS) & (mixed % SLOTS == plain % SLOTS)
    return jnp.where(same & (mixed // SLOTS % 2 == half), 1.0, 0.0).astype(BF16)


def unmix_kernel(mixed_ref, rows_ref):
    width = mixed_ref.shape[1]
    mixed = mixed_ref[...]
    for h in range(2):
        part = dot(half_matrix(rows_ref.shape[0], h, False), mixed)
        rows_ref[:, h * width : (h + 1) * width] = part.astype(BF16)


def first_kernel(core_ref, *refs):
    *pieces, gate_own, gate_far, up_own, up_far, down_own, down_far, act_ref = refs
    units = gate_own.shape[1]
    rows = pieces[0].shape[0]

    @pl.when(core_ref[0] == 0)
    def _():
        for i, piece in enumerate(pieces):
            x = piece[...]
            for j, (gate, up) in enumerate(((gate_own, up_own), (gate_far, up_far))):
                gate_proj = dot(x, gate[...])
                up_proj = dot(x, up[...])
                sig = jax.nn.sigmoid(gate_proj)
                active = gate_proj * sig
                slope = up_proj * sig * (1.0 + gate_proj * (1.0 - sig))
                for k, value in enumerate((slope, active, active * up_proj)):
                    start = (2 * k + j) * units
                    act_ref[i * rows : (i + 1) * rows, start : start + units] = value.astype(BF16)

    @pl.when(core_ref[0] != 0)
    def _():
        for i, piece in enumerate(pieces):
            dy = piece[...]
            for j, down in enumerate((down_far, down_own)):
                value = dot(dy, down[...], 1, 1).astype(BF16)
                for k in range(2):
                    start = (2 * k + j) * units
                    act_ref[i * rows : (i + 1) * rows, start : start + units] = value
                start = (4 + j) * units
                act_ref[i * rows : (i + 1) * rows, start : start + units] = jnp.ones_like(value)


def block_of(refs, line, inner, rows):
    ref = refs[(0, 1, 1, 2)[line]]
    start = ((0, 0, 1, 0)[line] * SIDE + inner) * rows
    return ref[start : start + rows, :]


def line_product(mine, far, line, rows):
    return jnp.concatenate(
        [
            block_of(mine, line, inner, rows) * block_of(far, inner, line, rows)
            for inner in range(SIDE)
        ],
        axis=0,
    )


def second(core_ref, product, weights, stores):
    gate_own, gate_far, up_own, up_far, down_own, down_far = weights
    units = gate_own.shape[1]
    width = down_own.shape[1]
    step = 512
    half = product.shape[0] // 2

    @pl.when(core_ref[0] == 0)
    def _():
        for c in range(0, width, step):
            total = dot(product[:, 4 * units : 5 * units], down_own[:, c : c + step]) + dot(
                product[:, 5 * units :], down_far[:, c : c + step]
            )
            for i, ref in enumerate(stores):
                ref[:, c : c + step] = total[i * half : (i + 1) * half].astype(BF16)

    @pl.when(core_ref[0] != 0)
    def _():
        for c in range(0, width, step):
            total = dot(product[:, :units], gate_far[c : c + step, :], 1, 1)
            for k, ref in enumerate((gate_own, up_far, up_own)):
                part = product[:, (k + 1) * units : (k + 2) * units]
                total = total + dot(part, ref[c : c + step, :], 1, 1)
            for i, ref in enumerate(stores):
                ref[:, c : c + step] = total[i * half : (i + 1) * half].astype(BF16)


def far_line_kernel(rows, core_ref, *refs):
    mine, far, weights, stores = refs[:3], refs[3:6], refs[6:12], refs[12:]
    second(core_ref, line_product(mine, far, 3, rows), weights, stores)


def other_lines_kernel(rows, core_ref, *refs):
    mine, far, weights, stores, act = refs[:3], refs[3:6], refs[6:12], refs[12:18], refs[18]
    for line in range(SIDE):
        product = line_product(mine, far, line, rows)
        act[line * SIDE * rows : (line + 1) * SIDE * rows, :] = product
        if line < 3:
            second(core_ref, product, weights, stores[2 * line : 2 * line + 2])


def grads_kernel(core_ref, *refs):
    *pieces, act, keep_gate, keep_up, keep_down, send_first, send_second = refs
    units = keep_gate.shape[1]
    step = 256
    blocks = keep_down.shape[1] // step

    def column(c):
        return jnp.concatenate([p[:, pl.ds(c, step)] for p in pieces], axis=0)

    @pl.when(core_ref[0] == 0)
    def _():
        def one(i, carry):
            c = pl.multiple_of(i * step, step)
            total = dot(column(c), act[:, : 4 * units], 0, 0).astype(BF16)
            for k, ref in enumerate((keep_gate, send_first, keep_up, send_second)):
                ref[pl.ds(c, step), :] = total[:, k * units : (k + 1) * units]
            return carry

        lax.fori_loop(0, blocks, one, 0)

    @pl.when(core_ref[0] != 0)
    def _():
        def one(i, carry):
            c = pl.multiple_of(i * step, step)
            total = dot(act[:, 4 * units :], column(c), 0, 0).astype(BF16)
            send_first[pl.ds(c, step), :] = total[:units]
            keep_down[:, pl.ds(c, step)] = total[units:]
            return carry

        lax.fori_loop(0, blocks, one, 0)


def settle_kernel(
    core_ref, keep_gate, keep_up, keep_down, got_first, got_second, gate_ref, up_ref, down_ref
):
    units = keep_gate.shape[1]

    @pl.when(core_ref[0] == 0)
    def _():
        gate_ref[...] = keep_gate[...]
        up_ref[...] = keep_up[...]
        for c in range(0, keep_down.shape[1], units):
            down_ref[:, c : c + units] = got_first[c : c + units, :]

    @pl.when(core_ref[0] != 0)
    def _():
        gate_ref[...] = got_first[...]
        up_ref[...] = got_second[...]
        down_ref[...] = keep_down[...]


def add(*parts):
    total = parts[0].astype(F32)
    for part in parts[1:]:
        total = total + part.astype(F32)
    return total.astype(BF16)


def line_sum_kernel(*refs):
    low, high, outs = refs[:3], refs[3:6], refs[6:]
    rows = outs[0].shape[0]
    for i, group in enumerate((low, high)):
        for j in range(2):
            at = slice(j * rows, (j + 1) * rows)
            outs[2 * i + j][...] = add(*[r[at, :] for r in group])


def home_kernel(own, one, two, three, mixed_ref):
    rows, width = own.shape
    total = add(own[...], one[...], two[...], three[...])
    low = dot(half_matrix(rows, 0, True), total[:, : width // 2])
    high = dot(half_matrix(rows, 1, True), total[:, width // 2 :])
    mixed_ref[...] = (low + high).astype(BF16)


def body(tokens, expert_ids, gate_values, cotangent, w_gate, w_up, w_down):
    tok_rows, width = tokens.shape
    experts = lax.axis_size("expert")
    sources = 2 * experts
    rows = sources * SLOTS
    units = w_gate.shape[2]
    core = lax.axis_index("dp").astype(jnp.int32).reshape(1)
    ids, gates = expert_ids.T, gate_values.T

    weights = []
    for own in (w_gate[0], w_up[0], w_down[0]):
        weights += [own, swap(own)]

    send = call(functools.partial(dispatch_kernel, experts), shape(2 * rows, width // 2))(
        ids, gates, tokens, cotangent
    )
    mixed = exchange(send, sources)
    mine = call(unmix_kernel, shape(rows, width))(mixed)

    plus = shift(mine, -1, False)
    minus = shift(mine, 1, False)
    far = shift(mine, 2, False)
    low = jnp.concatenate([mine, plus], axis=0)
    high = jnp.concatenate([minus, far], axis=0)
    low_minus = shift(low, 1, True)
    high_plus = shift(high, -1, True)
    high_minus = shift(high, 1, True)
    low_plus = shift(low, -1, True)
    low_far = shift(low_minus, 1, True)
    high_far = shift(high_plus, -1, True)
    line = SIDE * rows
    groups = ((low, high), (low_plus, high_plus, low_minus, high_minus), (low_far, high_far))

    acts = []
    for group in groups:
        count = len(group) * line // 2
        acts.append(
            call(first_kernel, shape(count, 6 * units), flops=8 * count * width * units)(
                core, *group, *weights
            )
        )
    far_acts = [swap(a) for a in acts]

    half = shape(line // 2, width)
    out_low_far, out_high_far = call(
        functools.partial(far_line_kernel, rows), (half, half), flops=8 * line * width * units
    )(core, *acts, *far_acts, *weights)
    low_got = shift(out_low_far, -1, True)
    high_got = shift(out_high_far, 1, True)
    *outs, act = call(
        functools.partial(other_lines_kernel, rows),
        (half,) * 6 + (shape(SIDE * line, 6 * units),),
        flops=24 * line * width * units,
    )(core, *acts, *far_acts, *weights)
    out_low, out_high, out_low_plus, out_high_plus, out_low_minus, out_high_minus = outs
    high_one = shift(out_high_minus, -1, True)
    low_one = shift(out_low_plus, 1, True)
    low_two = shift(add(out_low_minus, low_got), -1, True)
    high_two = shift(add(out_high_plus, high_got), 1, True)
    block = shape(rows, width)
    own, plus_sum, minus_sum, far_sum = call(line_sum_kernel, (block,) * 4)(
        out_low, low_one, low_two, out_high, high_one, high_two
    )
    got_plus = shift(plus_sum, 1, False)
    got_minus = shift(minus_sum, -1, False)
    got_far = shift(far_sum, 2, False)
    back = call(home_kernel, shape(2 * rows, width // 2))(own, got_plus, got_minus, got_far)
    home = exchange(back, sources)
    token_shape = shape(tok_rows, width)
    moe_out, d_tokens = call(
        functools.partial(combine_kernel, experts), (token_shape, token_shape)
    )(ids, gates, home)

    column, flat = shape(width, units), shape(units, width)
    keep_gate, keep_up, keep_down, send_first, send_second = call(
        grads_kernel,
        (column, column, flat, column, column),
        flops=32 * line * width * units,
    )(core, *groups[0], *groups[1], *groups[2], act)
    got_first, got_second = swap(send_first), swap(send_second)
    d_gate, d_up, d_down = call(settle_kernel, (column, column, flat))(
        core, keep_gate, keep_up, keep_down, got_first, got_second
    )
    return moe_out, d_tokens, d_gate[None], d_up[None], d_down[None]


def solution(mesh):
    token_spec = P(("dp", "expert", "tensor"), None)
    column_spec = P("expert", None, ("dp", "tensor"))
    row_spec = P("expert", ("dp", "tensor"), None)
    in_specs = (token_spec,) * 4 + (column_spec, column_spec, row_spec)
    out_specs = (token_spec, token_spec, column_spec, column_spec, row_spec)
    return jax.shard_map(body, mesh=mesh, in_specs=in_specs, out_specs=out_specs, check_vma=False)
```

```python
import functools

import jax
import jax.numpy as jnp
from jax import lax
from jax.experimental import pallas as pl
from jax.experimental.pallas import tpu as pltpu
from jax.sharding import PartitionSpec as P

BF16 = jnp.bfloat16
F32 = jnp.float32
SIDE = 4
SLOTS = 4
MIB = 1024 * 1024
IN_VMEM = pl.BlockSpec(memory_space=pltpu.VMEM)
IN_SMEM = pl.BlockSpec(memory_space=pltpu.SMEM)
IN_ANY = pl.BlockSpec(memory_space=pl.ANY)


def dot(left, right, left_dim=1, right_dim=0):
    return lax.dot_general(
        left, right, (((left_dim,), (right_dim,)), ((), ())), preferred_element_type=F32
    )


def call(kernel, out_shape, flops=0, limit=16, after=(), scratch=()):
    def run(*args):
        specs = [IN_SMEM if a.shape == (1,) else IN_VMEM for a in args]
        outs = jax.tree.map(lambda _: IN_VMEM, out_shape)
        count = len(args)

        def inner(*refs):
            kernel(*refs[:count], *refs[count + len(after) :])

        return pl.pallas_call(
            inner,
            out_shape=out_shape,
            in_specs=specs + [IN_ANY] * len(after),
            out_specs=outs,
            scratch_shapes=scratch,
            cost_estimate=pl.CostEstimate(flops=flops, bytes_accessed=0, transcendentals=0),
            compiler_params=pltpu.CompilerParams(vmem_limit_bytes=limit * MIB),
        )(*args, *after)

    return run


def tie(values, after):
    count = len(values)

    def nothing(*refs):
        pass

    return pl.pallas_call(
        nothing,
        out_shape=[jax.ShapeDtypeStruct(v.shape, v.dtype) for v in values],
        in_specs=[IN_ANY] * (count + len(after)),
        out_specs=[IN_ANY] * count,
        input_output_aliases={i: i for i in range(count)},
    )(*values, *after)


def shape(*dims):
    return jax.ShapeDtypeStruct(dims, BF16)


def shift(block, step, second):
    pairs = []
    for core in range(2):
        for y in range(SIDE):
            for x in range(SIDE):
                if (core == 0) != second:
                    target = y * SIDE + (x + step) % SIDE
                else:
                    target = (y + step) % SIDE * SIDE + x
                base = core * SIDE * SIDE
                pairs.append((base + y * SIDE + x, base + target))
    return lax.ppermute(block, ("dp", "tensor"), pairs)


def swap(block):
    return lax.ppermute(block, "dp", [(0, 1), (1, 0)])


def exchange(rows, parts):
    blocks = rows.reshape(parts, rows.shape[0] // parts, rows.shape[1])
    moved = lax.all_to_all(blocks, ("dp", "expert"), split_axis=0, concat_axis=0, tiled=True)
    return moved.reshape(rows.shape)


def spread(ids, gates, experts):
    tokens = ids.shape[1]
    dims = (experts * 2 * SLOTS, tokens)
    row = lax.broadcasted_iota(jnp.int32, dims, 0)
    expert, half, slot = row // (2 * SLOTS), row // SLOTS % 2, row % SLOTS
    first, second = ids[0:1, :] == expert, ids[1:2, :] == expert
    named = jnp.where(first | second, 1.0, 0.0).astype(F32)
    earlier = lax.broadcasted_iota(jnp.int32, (tokens, tokens), 0)
    later = lax.broadcasted_iota(jnp.int32, (tokens, tokens), 1)
    place = dot(named, jnp.where(earlier < later, 1.0, 0.0).astype(F32))
    select = jnp.where(place == slot.astype(F32), named, 0.0)
    weight = jnp.where(first, gates[0:1, :], 0.0) + jnp.where(second, gates[1:2, :], 0.0)
    weighted = select * weight
    return (
        [jnp.where(half == h, select, 0.0) for h in range(2)],
        [jnp.where(half == h, weighted, 0.0) for h in range(2)],
    )


def dispatch_kernel(experts, *refs):
    sources, send_ref, buffers, sems = refs[:4], refs[4], refs[5:9], refs[9]
    copies = [
        pltpu.make_async_copy(source, buffer, sems.at[i])
        for i, (source, buffer) in enumerate(zip(sources, buffers))
    ]
    for copy in copies:
        copy.start()
    for copy in copies:
        copy.wait()
    ids_ref, gates_ref, tokens_ref, cotangent_ref = buffers
    select, weighted = spread(ids_ref[...], gates_ref[...].astype(F32), experts)
    width = tokens_ref.shape[1] // 2
    rows = experts * 2 * SLOTS
    for mats, ref, start in ((select, tokens_ref, 0), (weighted, cotangent_ref, rows)):
        total = dot(mats[0], ref[:, :width].astype(F32)) + dot(
            mats[1], ref[:, width:].astype(F32)
        )
        send_ref[start : start + rows, :] = total.astype(BF16)


def dispatch(experts, *args):
    rows = 4 * experts * SLOTS
    return pl.pallas_call(
        functools.partial(dispatch_kernel, experts),
        out_shape=shape(rows, args[2].shape[1] // 2),
        in_specs=[IN_ANY] * 4,
        out_specs=IN_VMEM,
        scratch_shapes=[pltpu.VMEM(a.shape, a.dtype) for a in args]
        + [pltpu.SemaphoreType.DMA((4,))],
        compiler_params=pltpu.CompilerParams(vmem_limit_bytes=16 * MIB),
    )(*args)


def combine_kernel(experts, ids_ref, gates_ref, home_ref, out_ref, back_ref):
    select, weighted = spread(ids_ref[...], gates_ref[...].astype(F32), experts)
    width = out_ref.shape[1] // 2
    rows = experts * 2 * SLOTS
    for mats, ref, start in ((weighted, out_ref, 0), (select, back_ref, rows)):
        part = home_ref[start : start + rows, :].astype(F32)
        for h in range(2):
            ref[:, h * width : (h + 1) * width] = dot(mats[h], part, 0, 0).astype(BF16)


def half_matrix(rows, half, flip):
    dims = (2 * rows, rows) if flip else (rows, 2 * rows)
    plain = lax.broadcasted_iota(jnp.int32, dims, 1 if flip else 0)
    mixed = lax.broadcasted_iota(jnp.int32, dims, 0 if flip else 1)
    same = (mixed // (2 * SLOTS) == plain // SLOTS) & (mixed % SLOTS == plain % SLOTS)
    return jnp.where(same & (mixed // SLOTS % 2 == half), 1.0, 0.0).astype(BF16)


def unmix_kernel(mixed_ref, rows_ref):
    width = mixed_ref.shape[1]
    mixed = mixed_ref[...]
    for h in range(2):
        part = dot(half_matrix(rows_ref.shape[0], h, False), mixed)
        rows_ref[:, h * width : (h + 1) * width] = part.astype(BF16)


def first_kernel(core_ref, *refs):
    *pieces, gate_own, gate_far, up_own, up_far, down_own, down_far, act_ref = refs
    units = gate_own.shape[1]
    rows = pieces[0].shape[0]

    @pl.when(core_ref[0] == 0)
    def _():
        for i in range(0, len(pieces), 2):
            x = jnp.concatenate([p[...] for p in pieces[i : i + 2]], axis=0)
            at = slice(i * rows, (i + 2) * rows)
            for j, (gate, up) in enumerate(((gate_own, up_own), (gate_far, up_far))):
                gate_proj = dot(x, gate[...])
                up_proj = dot(x, up[...])
                sig = jax.nn.sigmoid(gate_proj)
                active = gate_proj * sig
                slope = up_proj * sig * (1.0 + gate_proj * (1.0 - sig))
                for k, value in enumerate((slope, active, active * up_proj)):
                    start = (2 * k + j) * units
                    act_ref[at, start : start + units] = value.astype(BF16)

    @pl.when(core_ref[0] != 0)
    def _():
        for i in range(0, len(pieces), 2):
            dy = jnp.concatenate([p[...] for p in pieces[i : i + 2]], axis=0)
            at = slice(i * rows, (i + 2) * rows)
            for j, down in enumerate((down_far, down_own)):
                value = dot(dy, down[...], 1, 1).astype(BF16)
                for k in range(2):
                    start = (2 * k + j) * units
                    act_ref[at, start : start + units] = value
                start = (4 + j) * units
                act_ref[at, start : start + units] = jnp.ones_like(value)


def block_of(refs, line, inner, rows):
    ref = refs[(0, 1, 1, 2)[line]]
    start = ((0, 0, 1, 0)[line] * SIDE + inner) * rows
    return ref[start : start + rows, :]


def line_product(mine, far, line, rows):
    return jnp.concatenate(
        [
            block_of(mine, line, inner, rows) * block_of(far, inner, line, rows)
            for inner in range(SIDE)
        ],
        axis=0,
    )


def second(core_ref, product, weights, stores):
    gate_own, gate_far, up_own, up_far, down_own, down_far = weights
    units = gate_own.shape[1]
    width = down_own.shape[1]
    step = 512
    half = product.shape[0] // 2

    @pl.when(core_ref[0] == 0)
    def _():
        for c in range(0, width, step):
            total = dot(product[:, 4 * units : 5 * units], down_own[:, c : c + step]) + dot(
                product[:, 5 * units :], down_far[:, c : c + step]
            )
            for i, ref in enumerate(stores):
                ref[:, c : c + step] = total[i * half : (i + 1) * half].astype(BF16)

    @pl.when(core_ref[0] != 0)
    def _():
        for c in range(0, width, step):
            total = dot(product[:, :units], gate_far[c : c + step, :], 1, 1)
            for k, ref in enumerate((gate_own, up_far, up_own)):
                part = product[:, (k + 1) * units : (k + 2) * units]
                total = total + dot(part, ref[c : c + step, :], 1, 1)
            for i, ref in enumerate(stores):
                ref[:, c : c + step] = total[i * half : (i + 1) * half].astype(BF16)


def lines_kernel(rows, lines, core_ref, *refs):
    mine, far, weights, stores = refs[:3], refs[3:6], refs[6:12], refs[12:]
    for i, line in enumerate(lines):
        product = line_product(mine, far, line, rows)
        second(core_ref, product, weights, stores[2 * i : 2 * i + 2])


def own_line_kernel(rows, core_ref, *refs):
    mine, far, weights, stores, act = refs[:3], refs[3:6], refs[6:12], refs[12:14], refs[14]
    for line in range(SIDE):
        product = line_product(mine, far, line, rows)
        act[line * SIDE * rows : (line + 1) * SIDE * rows, :] = product
        if line == 0:
            second(core_ref, product, weights, stores)


STEP = 256


def column(pieces, c):
    return jnp.concatenate([p[:, pl.ds(c, STEP)] for p in pieces], axis=0)


def grads_kernel(final, core_ref, *refs):
    if final:
        *pieces, act, keep, keep_down, send = refs
    else:
        *pieces, act, keep, send = refs
    units = keep.shape[1]
    blocks = keep.shape[0] // STEP

    @pl.when(core_ref[0] == 0)
    def _():
        first = 2 * units * final

        def one(i, carry):
            c = pl.multiple_of(i * STEP, STEP)
            total = dot(column(pieces, c), act[:, first : first + 2 * units], 0, 0).astype(BF16)
            keep[pl.ds(c, STEP), :] = total[:, :units]
            send[pl.ds(c, STEP), :] = total[:, units:]
            return carry

        lax.fori_loop(0, blocks, one, 0)

    @pl.when(core_ref[0] != 0)
    def _():
        first = (4 + final) * units

        def one(i, carry):
            c = pl.multiple_of(i * STEP, STEP)
            total = dot(act[:, first : first + units], column(pieces, c), 0, 0).astype(BF16)
            if final:
                keep_down[:, pl.ds(c, STEP)] = total
            else:
                send[pl.ds(c, STEP), :] = total
            return carry

        lax.fori_loop(0, blocks, one, 0)


def settle_kernel(
    core_ref, keep_gate, keep_up, keep_down, got_first, got_second, gate_ref, up_ref, down_ref
):
    units = keep_gate.shape[1]

    @pl.when(core_ref[0] == 0)
    def _():
        gate_ref[...] = keep_gate[...]
        up_ref[...] = keep_up[...]
        for c in range(0, keep_down.shape[1], units):
            down_ref[:, c : c + units] = got_first[c : c + units, :]

    @pl.when(core_ref[0] != 0)
    def _():
        gate_ref[...] = got_first[...]
        up_ref[...] = got_second[...]
        down_ref[...] = keep_down[...]


def add(*parts):
    total = parts[0].astype(F32)
    for part in parts[1:]:
        total = total + part.astype(F32)
    return total.astype(BF16)


def line_sum_kernel(*refs):
    low, high, outs = refs[:3], refs[3:6], refs[6:]
    rows = outs[0].shape[0]
    for i, group in enumerate((low, high)):
        for j in range(2):
            at = slice(j * rows, (j + 1) * rows)
            outs[2 * i + j][...] = add(*[r[at, :] for r in group])


def home_kernel(own, one, two, three, mixed_ref):
    rows, width = own.shape
    total = add(own[...], one[...], two[...], three[...])
    low = dot(half_matrix(rows, 0, True), total[:, : width // 2])
    high = dot(half_matrix(rows, 1, True), total[:, width // 2 :])
    mixed_ref[...] = (low + high).astype(BF16)


def body(tokens, expert_ids, gate_values, cotangent, w_gate, w_up, w_down):
    tok_rows, width = tokens.shape
    experts = lax.axis_size("expert")
    sources = 2 * experts
    rows = sources * SLOTS
    units = w_gate.shape[2]
    core = lax.axis_index("dp").astype(jnp.int32).reshape(1)
    ids, gates = expert_ids.T, gate_values.T

    weights = []
    for own in (w_gate[0], w_up[0], w_down[0]):
        weights += [own, swap(own)]

    send = dispatch(experts, ids, gates, tokens, cotangent)
    mixed = exchange(send, sources)
    mine = call(unmix_kernel, shape(rows, width), after=weights[1::2])(mixed)

    plus = shift(mine, -1, False)
    minus = shift(mine, 1, False)
    far = shift(mine, 2, False)
    low = jnp.concatenate([mine, plus], axis=0)
    high = jnp.concatenate([minus, far], axis=0)
    low_minus = shift(low, 1, True)
    high_plus = shift(high, -1, True)
    high_minus = shift(high, 1, True)
    low_plus = shift(low, -1, True)

    def first(*pieces):
        count = len(pieces) * pieces[0].shape[0]
        return call(
            first_kernel, shape(count, 6 * units), flops=8 * count * width * units, limit=28
        )(core, *pieces, *weights)

    act_own = first(low, high)
    low_minus, high_plus = tie((low_minus, high_plus), (act_own,))
    low_far = shift(low_minus, 1, True)
    high_far = shift(high_plus, -1, True)
    line = SIDE * rows
    acts = [
        act_own,
        first(low_plus, high_plus, low_minus, high_minus),
        first(low_far, high_far),
    ]
    far_acts = [swap(a) for a in acts]
    pieces = (low, high, low_plus, high_plus, low_minus, high_minus, low_far, high_far)

    half = shape(line // 2, width)

    def lines(*which):
        return call(
            functools.partial(lines_kernel, rows, which),
            (half,) * (2 * len(which)),
            flops=8 * len(which) * line * width * units,
            limit=28,
        )(core, *acts, *far_acts, *weights)

    out_low_far, out_high_far = lines(3)
    low_got = shift(out_low_far, -1, True)
    high_got = shift(out_high_far, 1, True)
    out_low_plus, out_high_plus, out_low_minus, out_high_minus = lines(1, 2)
    high_one = shift(out_high_minus, -1, True)
    low_one = shift(out_low_plus, 1, True)
    low_two = shift(add(out_low_minus, low_got), -1, True)
    high_two = shift(add(out_high_plus, high_got), 1, True)
    out_low, out_high, act = call(
        functools.partial(own_line_kernel, rows),
        (half, half, shape(SIDE * line, 6 * units)),
        flops=8 * line * width * units,
        limit=28,
    )(core, *acts, *far_acts, *weights)

    column_shape, flat_shape = shape(width, units), shape(units, width)
    keep_gate, send_first = call(
        functools.partial(grads_kernel, 0),
        (column_shape, column_shape),
        flops=16 * line * width * units,
        limit=28,
    )(core, *pieces, act)
    got_first = swap(send_first)

    block = shape(rows, width)
    own, plus_sum, minus_sum, far_sum = call(line_sum_kernel, (block,) * 4, after=(keep_gate,))(
        out_low, low_one, low_two, out_high, high_one, high_two
    )
    got_plus = shift(plus_sum, 1, False)
    got_minus = shift(minus_sum, -1, False)
    got_far = shift(far_sum, 2, False)
    back = call(home_kernel, shape(2 * rows, width // 2))(own, got_plus, got_minus, got_far)
    home = exchange(back, sources)

    keep_up, keep_down, send_second = call(
        functools.partial(grads_kernel, 1),
        (column_shape, flat_shape, column_shape),
        flops=16 * line * width * units,
        limit=28,
        after=(back,),
    )(core, *pieces, act)
    got_second = swap(send_second)
    d_gate, d_up, d_down = call(settle_kernel, (column_shape, column_shape, flat_shape), limit=28)(
        core, keep_gate, keep_up, keep_down, got_first, got_second
    )
    token_shape = shape(tok_rows, width)
    moe_out, d_tokens = call(
        functools.partial(combine_kernel, experts), (token_shape, token_shape)
    )(ids, gates, home)
    return moe_out, d_tokens, d_gate[None], d_up[None], d_down[None]


def solution(mesh):
    token_spec = P(("dp", "expert", "tensor"), None)
    column_spec = P("expert", None, ("dp", "tensor"))
    row_spec = P("expert", ("dp", "tensor"), None)
    in_specs = (token_spec,) * 4 + (column_spec, column_spec, row_spec)
    out_specs = (token_spec, token_spec, column_spec, column_spec, row_spec)
    return jax.shard_map(body, mesh=mesh, in_specs=in_specs, out_specs=out_specs, check_vma=False)
```

```python
import functools

import jax
import jax.numpy as jnp
from jax import lax
from jax.experimental import pallas as pl
from jax.experimental.pallas import tpu as pltpu
from jax.sharding import PartitionSpec as P

BF16 = jnp.bfloat16
F32 = jnp.float32
SIDE = 4
SLOTS = 4
MIB = 1024 * 1024
IN_VMEM = pl.BlockSpec(memory_space=pltpu.VMEM)
IN_ANY = pl.BlockSpec(memory_space=pl.ANY)


def dot(left, right, left_dim=1, right_dim=0):
    return lax.dot_general(
        left, right, (((left_dim,), (right_dim,)), ((), ())), preferred_element_type=F32
    )


def call(kernel, out_shape, micros=1, limit=16, after=()):
    def run(*args):
        specs = [IN_VMEM] * len(args)
        outs = jax.tree.map(lambda _: IN_VMEM, out_shape)
        count = len(args)

        def inner(*refs):
            kernel(*refs[:count], *refs[count + len(after) :])

        return pl.pallas_call(
            inner,
            out_shape=out_shape,
            in_specs=specs + [IN_ANY] * len(after),
            out_specs=outs,
            cost_estimate=pl.CostEstimate(
                flops=int(micros * FLOPS_IN_MICRO), bytes_accessed=0, transcendentals=0
            ),
            compiler_params=pltpu.CompilerParams(vmem_limit_bytes=limit * MIB),
        )(*args, *after)

    return run


def tie(values, after):
    count = len(values)

    def nothing(*refs):
        pass

    return pl.pallas_call(
        nothing,
        out_shape=[jax.ShapeDtypeStruct(v.shape, v.dtype) for v in values],
        in_specs=[IN_ANY] * (count + len(after)),
        out_specs=[IN_ANY] * count,
        input_output_aliases={i: i for i in range(count)},
        compiler_params=pltpu.CompilerParams(vmem_limit_bytes=MIB),
    )(*values, *after)


def shape(*dims):
    return jax.ShapeDtypeStruct(dims, BF16)


FLAG = shape(16, 128)
FLOPS_IN_MICRO = 1.15e7


def shift(block, step, second):
    pairs = []
    for core in range(2):
        for y in range(SIDE):
            for x in range(SIDE):
                if (core == 0) != second:
                    target = y * SIDE + (x + step) % SIDE
                else:
                    target = (y + step) % SIDE * SIDE + x
                base = core * SIDE * SIDE
                pairs.append((base + y * SIDE + x, base + target))
    return lax.ppermute(block, ("dp", "tensor"), pairs)


def swap(block):
    return lax.ppermute(block, "dp", [(0, 1), (1, 0)])


def exchange(rows, parts):
    blocks = rows.reshape(parts, rows.shape[0] // parts, rows.shape[1])
    moved = lax.all_to_all(blocks, ("dp", "expert"), split_axis=0, concat_axis=0, tiled=True)
    return moved.reshape(rows.shape)


def spread(ids, gates, experts):
    tokens = ids.shape[1]
    dims = (experts * 2 * SLOTS, tokens)
    row = lax.broadcasted_iota(jnp.int32, dims, 0)
    expert, half, slot = row // (2 * SLOTS), row // SLOTS % 2, row % SLOTS
    first, second = ids[0:1, :] == expert, ids[1:2, :] == expert
    named = jnp.where(first | second, 1.0, 0.0).astype(F32)
    earlier = lax.broadcasted_iota(jnp.int32, (tokens, tokens), 0)
    later = lax.broadcasted_iota(jnp.int32, (tokens, tokens), 1)
    place = dot(named, jnp.where(earlier < later, 1.0, 0.0).astype(F32))
    select = jnp.where(place == slot.astype(F32), named, 0.0)
    weight = jnp.where(first, gates[0:1, :], 0.0) + jnp.where(second, gates[1:2, :], 0.0)
    weighted = select * weight
    return (
        [jnp.where(half == h, select, 0.0) for h in range(2)],
        [jnp.where(half == h, weighted, 0.0) for h in range(2)],
    )


def dispatch_kernel(experts, *refs):
    sources, send_ref, buffers, sems = refs[:4], refs[4], refs[5:9], refs[9]
    copies = [
        pltpu.make_async_copy(source, buffer, sems.at[i])
        for i, (source, buffer) in enumerate(zip(sources, buffers))
    ]
    for copy in copies:
        copy.start()
    for copy in copies:
        copy.wait()
    ids_ref, gates_ref, tokens_ref, cotangent_ref = buffers
    select, weighted = spread(ids_ref[...], gates_ref[...].astype(F32), experts)
    width = tokens_ref.shape[1] // 2
    rows = experts * 2 * SLOTS
    for mats, ref, start in ((select, tokens_ref, 0), (weighted, cotangent_ref, rows)):
        total = dot(mats[0], ref[:, :width].astype(F32)) + dot(
            mats[1], ref[:, width:].astype(F32)
        )
        send_ref[start : start + rows, :] = total.astype(BF16)


def dispatch(experts, *args):
    rows = 4 * experts * SLOTS
    return pl.pallas_call(
        functools.partial(dispatch_kernel, experts),
        out_shape=shape(rows, args[2].shape[1] // 2),
        in_specs=[IN_ANY] * 4,
        out_specs=IN_VMEM,
        scratch_shapes=[pltpu.VMEM(a.shape, a.dtype) for a in args]
        + [pltpu.SemaphoreType.DMA((4,))],
        compiler_params=pltpu.CompilerParams(vmem_limit_bytes=16 * MIB),
    )(*args)


def combine_kernel(experts, ids_ref, gates_ref, home_ref, out_ref, back_ref):
    select, weighted = spread(ids_ref[...], gates_ref[...].astype(F32), experts)
    width = out_ref.shape[1] // 2
    rows = experts * 2 * SLOTS
    for mats, ref, start in ((weighted, out_ref, 0), (select, back_ref, rows)):
        part = home_ref[start : start + rows, :].astype(F32)
        for h in range(2):
            ref[:, h * width : (h + 1) * width] = dot(mats[h], part, 0, 0).astype(BF16)


def half_matrix(rows, half, flip):
    dims = (2 * rows, rows) if flip else (rows, 2 * rows)
    plain = lax.broadcasted_iota(jnp.int32, dims, 1 if flip else 0)
    mixed = lax.broadcasted_iota(jnp.int32, dims, 0 if flip else 1)
    same = (mixed // (2 * SLOTS) == plain // SLOTS) & (mixed % SLOTS == plain % SLOTS)
    return jnp.where(same & (mixed // SLOTS % 2 == half), 1.0, 0.0).astype(BF16)


def unmix_kernel(mixed_ref, rows_ref):
    width = mixed_ref.shape[1]
    mixed = mixed_ref[...]
    for h in range(2):
        part = dot(half_matrix(rows_ref.shape[0], h, False), mixed)
        rows_ref[:, h * width : (h + 1) * width] = part.astype(BF16)


def load_kernel(*refs):
    for source, target in zip(refs[:3], refs[3:6]):
        target[...] = source[...]
    refs[6][...] = jnp.zeros_like(refs[6])


def join_kernel(top_ref, bottom_ref, rows_ref):
    rows = top_ref.shape[0]
    rows_ref[:rows, :] = top_ref[...]
    rows_ref[rows:, :] = bottom_ref[...]


def first_kernel(*refs):
    *pieces, gate_own, gate_far, up_own, up_far, down_own, down_far, act_ref = refs
    units = gate_own.shape[1]
    rows = pieces[0].shape[0]

    @pl.when(lax.axis_index("dp") == 0)
    def _():
        for i in range(0, len(pieces), 2):
            x = jnp.concatenate([p[...] for p in pieces[i : i + 2]], axis=0)
            at = slice(i * rows, (i + 2) * rows)
            for j, (gate, up) in enumerate(((gate_own, up_own), (gate_far, up_far))):
                gate_proj = dot(x, gate[...])
                up_proj = dot(x, up[...])
                sig = jax.nn.sigmoid(gate_proj)
                active = gate_proj * sig
                slope = up_proj * sig * (1.0 + gate_proj * (1.0 - sig))
                for k, value in enumerate((slope, active, active * up_proj)):
                    start = (2 * k + j) * units
                    act_ref[at, start : start + units] = value.astype(BF16)

    @pl.when(lax.axis_index("dp") != 0)
    def _():
        for i in range(0, len(pieces), 2):
            dy = jnp.concatenate([p[...] for p in pieces[i : i + 2]], axis=0)
            at = slice(i * rows, (i + 2) * rows)
            for j, down in enumerate((down_far, down_own)):
                value = dot(dy, down[...], 1, 1).astype(BF16)
                for k in range(2):
                    start = (2 * k + j) * units
                    act_ref[at, start : start + units] = value
                start = (4 + j) * units
                act_ref[at, start : start + units] = jnp.ones_like(value)


def block_of(refs, line, inner, rows):
    ref = refs[(0, 1, 1, 2)[line]]
    start = ((0, 0, 1, 0)[line] * SIDE + inner) * rows
    return ref[start : start + rows, :]


def line_product(mine, far, line, rows):
    return jnp.concatenate(
        [
            block_of(mine, line, inner, rows) * block_of(far, inner, line, rows)
            for inner in range(SIDE)
        ],
        axis=0,
    )


def second(product, weights, stores):
    gate_own, gate_far, up_own, up_far, down_own, down_far = weights
    units = gate_own.shape[1]
    width = down_own.shape[1]
    step = 512
    half = product.shape[0] // 2

    @pl.when(lax.axis_index("dp") == 0)
    def _():
        for c in range(0, width, step):
            total = dot(product[:, 4 * units : 5 * units], down_own[:, c : c + step]) + dot(
                product[:, 5 * units :], down_far[:, c : c + step]
            )
            for i, ref in enumerate(stores):
                ref[:, c : c + step] = total[i * half : (i + 1) * half].astype(BF16)

    @pl.when(lax.axis_index("dp") != 0)
    def _():
        for c in range(0, width, step):
            total = dot(product[:, :units], gate_far[c : c + step, :], 1, 1)
            for k, ref in enumerate((gate_own, up_far, up_own)):
                part = product[:, (k + 1) * units : (k + 2) * units]
                total = total + dot(part, ref[c : c + step, :], 1, 1)
            for i, ref in enumerate(stores):
                ref[:, c : c + step] = total[i * half : (i + 1) * half].astype(BF16)


def lines_kernel(rows, lines, *refs):
    mine, far, weights, stores, flag = refs[:3], refs[3:6], refs[6:12], refs[12:-1], refs[-1]
    flag[...] = jnp.zeros_like(flag)
    for i, line in enumerate(lines):
        product = line_product(mine, far, line, rows)
        second(product, weights, stores[2 * i : 2 * i + 2])


def own_line_kernel(rows, *refs):
    mine, far, weights, stores, act = refs[:3], refs[3:6], refs[6:12], refs[12:14], refs[14]
    for line in range(SIDE):
        product = line_product(mine, far, line, rows)
        act[line * SIDE * rows : (line + 1) * SIDE * rows, :] = product
        if line == 0:
            second(product, weights, stores)


STEP = 256


def column(pieces, at):
    return jnp.concatenate([p[:, at] for p in pieces], axis=0)


def columns_loop(width, body):
    def one(i, carry):
        body(pl.ds(pl.multiple_of(i * STEP, STEP), STEP))
        return carry

    lax.fori_loop(0, width // STEP, one, 0)


def far_grads_kernel(*refs):
    *pieces, act, send, send_more, flag = refs
    units = send.shape[1]
    flag[...] = jnp.zeros_like(flag)

    @pl.when(lax.axis_index("dp") == 0)
    def _():
        factor = jnp.concatenate(
            [act[:, units : 2 * units], act[:, 3 * units : 4 * units]], axis=1
        )

        def one(at):
            total = dot(column(pieces, at), factor, 0, 0).astype(BF16)
            send[at, :] = total[:, :units]
            send_more[at, :] = total[:, units:]

        columns_loop(send.shape[0], one)

    @pl.when(lax.axis_index("dp") != 0)
    def _():
        hidden = act[:, 4 * units : 5 * units].T

        def one(at):
            send[at, :] = dot(hidden, column(pieces, at)).astype(BF16)

        columns_loop(send.shape[0], one)


def own_grads_kernel(*refs):
    *pieces, act, got, got_more, gate_ref, up_ref, down_ref = refs
    units = gate_ref.shape[1]
    width = gate_ref.shape[0]

    @pl.when(lax.axis_index("dp") == 0)
    def _():
        factor = jnp.concatenate([act[:, :units], act[:, 2 * units : 3 * units]], axis=1)

        def one(at):
            total = dot(column(pieces, at), factor, 0, 0).astype(BF16)
            gate_ref[at, :] = total[:, :units]
            up_ref[at, :] = total[:, units:]
            down_ref[:, at] = got[at, :]

        columns_loop(width, one)

    @pl.when(lax.axis_index("dp") != 0)
    def _():
        hidden = act[:, 5 * units :].T

        def one(at):
            down_ref[:, at] = dot(hidden, column(pieces, at)).astype(BF16)
            gate_ref[at, :] = got[at, :]
            up_ref[at, :] = got_more[at, :]

        columns_loop(width, one)


def add(*parts):
    total = parts[0].astype(F32)
    for part in parts[1:]:
        total = total + part.astype(F32)
    return total.astype(BF16)


def relay_sum_kernel(low, low_got, high, high_got, low_sum, high_sum, flag):
    low_sum[...] = add(low[...], low_got[...])
    high_sum[...] = add(high[...], high_got[...])
    flag[...] = jnp.zeros_like(flag)


def line_sum_kernel(*refs):
    low, high, outs = refs[:3], refs[3:6], refs[6:]
    rows = outs[0].shape[0]
    for i, group in enumerate((low, high)):
        for j in range(2):
            at = slice(j * rows, (j + 1) * rows)
            outs[2 * i + j][...] = add(*[r[at, :] for r in group])


def home_kernel(own, one, two, three, mixed_ref):
    rows, width = own.shape
    total = add(own[...], one[...], two[...], three[...])
    low = dot(half_matrix(rows, 0, True), total[:, : width // 2])
    high = dot(half_matrix(rows, 1, True), total[:, width // 2 :])
    mixed_ref[...] = (low + high).astype(BF16)


def body(tokens, expert_ids, gate_values, cotangent, w_gate, w_up, w_down):
    tok_rows, width = tokens.shape
    experts = lax.axis_size("expert")
    sources = 2 * experts
    rows = sources * SLOTS
    units = w_gate.shape[2]
    ids, gates = expert_ids.T, gate_values.T

    shards = (w_gate[0], w_up[0], w_down[0])
    others = [swap(w) for w in shards]

    rows_out = dispatch(experts, ids, gates, tokens, cotangent)
    mixed = exchange(rows_out, sources)
    mine = call(unmix_kernel, shape(rows, width), after=others)(mixed)

    plus = shift(mine, -1, False)
    minus = shift(mine, 1, False)
    far = shift(mine, 2, False)
    *owns, loaded = call(
        load_kernel, tuple(shape(*w.shape) for w in shards) + (FLAG,), after=(mine,)
    )(*shards)
    weights = [w for pair in zip(owns, others) for w in pair]
    low = call(join_kernel, shape(2 * rows, width), after=(loaded,))(mine, plus)
    high = call(join_kernel, shape(2 * rows, width))(minus, far)
    low_minus = shift(low, 1, True)
    high_plus = shift(high, -1, True)
    high_minus = shift(high, 1, True)
    low_plus = shift(low, -1, True)

    def first(*pieces):
        count = len(pieces) * pieces[0].shape[0]
        return call(
            first_kernel, shape(count, 6 * units), micros=count / 128, limit=18
        )(*pieces, *weights)

    act_own = first(low, high)
    low_minus, high_plus = tie((low_minus, high_plus), (act_own,))
    low_far = shift(low_minus, 1, True)
    high_far = shift(high_plus, -1, True)
    line = SIDE * rows
    acts = [
        act_own,
        first(low_plus, high_plus, low_minus, high_minus),
        first(low_far, high_far),
    ]
    far_acts = [swap(a) for a in acts]
    pieces = (low, high, low_plus, high_plus, low_minus, high_minus, low_far, high_far)

    half = shape(line // 2, width)

    def lines(*which):
        return call(
            functools.partial(lines_kernel, rows, which),
            (half,) * (2 * len(which)) + (FLAG,),
            micros=1.5 * len(which),
            limit=18,
        )(*acts, *far_acts, *weights)

    out_low_far, out_high_far, _ = lines(3)
    low_got = shift(out_low_far, -1, True)
    high_got = shift(out_high_far, 1, True)
    out_low_plus, out_high_plus, out_low_minus, out_high_minus, sides = lines(1, 2)
    high_one = shift(out_high_minus, -1, True)
    low_one = shift(out_low_plus, 1, True)
    low_sum, high_sum, relayed = call(relay_sum_kernel, (half, half, FLAG))(
        out_low_minus, low_got, out_high_plus, high_got
    )
    low_two, high_two = shift(low_sum, -1, True), shift(high_sum, 1, True)
    out_low, out_high, act = call(
        functools.partial(own_line_kernel, rows),
        (half, half, shape(SIDE * line, 6 * units)),
        micros=1.5,
        limit=18,
        after=(sides,),
    )(*acts, *far_acts, *weights)

    column_shape, flat_shape = shape(width, units), shape(units, width)
    send, send_more, sent = call(
        far_grads_kernel,
        (column_shape, column_shape, FLAG),
        micros=8,
        limit=18,
        after=(relayed,),
    )(*pieces, act)
    got, got_more = swap(send), swap(send_more)

    block = shape(rows, width)
    own, plus_sum, minus_sum, far_sum = call(line_sum_kernel, (block,) * 4, after=(sent,))(
        out_low, low_one, low_two, out_high, high_one, high_two
    )
    got_plus = shift(plus_sum, 1, False)
    got_minus = shift(minus_sum, -1, False)
    got_far = shift(far_sum, 2, False)
    back = call(home_kernel, shape(2 * rows, width // 2))(own, got_plus, got_minus, got_far)
    home = exchange(back, sources)
    d_gate, d_up, d_down = call(
        own_grads_kernel,
        (column_shape, column_shape, flat_shape),
        micros=13,
        limit=56,
        after=(back,),
    )(*pieces, act, got, got_more)
    token_shape = shape(tok_rows, width)
    moe_out, d_tokens = call(
        functools.partial(combine_kernel, experts), (token_shape, token_shape)
    )(ids, gates, home)
    return moe_out, d_tokens, d_gate[None], d_up[None], d_down[None]


def solution(mesh):
    token_spec = P(("dp", "expert", "tensor"), None)
    column_spec = P("expert", None, ("dp", "tensor"))
    row_spec = P("expert", ("dp", "tensor"), None)
    in_specs = (token_spec,) * 4 + (column_spec, column_spec, row_spec)
    out_specs = (token_spec, token_spec, column_spec, column_spec, row_spec)
    return jax.shard_map(body, mesh=mesh, in_specs=in_specs, out_specs=out_specs, check_vma=False)
```

```python
import functools

import jax
import jax.numpy as jnp
from jax import lax
from jax.experimental import pallas as pl
from jax.experimental.pallas import tpu as pltpu
from jax.sharding import PartitionSpec as P

BF16 = jnp.bfloat16
F32 = jnp.float32
SIDE = 4
SLOTS = 4
MIB = 1024 * 1024
IN_VMEM = pl.BlockSpec(memory_space=pltpu.VMEM)
IN_ANY = pl.BlockSpec(memory_space=pl.ANY)


def dot(left, right, left_dim=1, right_dim=0):
    return lax.dot_general(
        left, right, (((left_dim,), (right_dim,)), ((), ())), preferred_element_type=F32
    )


def call(kernel, out_shape, micros=1, limit=16, after=()):
    def run(*args):
        specs = [IN_VMEM] * len(args)
        outs = jax.tree.map(lambda _: IN_VMEM, out_shape)
        count = len(args)

        def inner(*refs):
            kernel(*refs[:count], *refs[count + len(after) :])

        return pl.pallas_call(
            inner,
            out_shape=out_shape,
            in_specs=specs + [IN_ANY] * len(after),
            out_specs=outs,
            cost_estimate=pl.CostEstimate(
                flops=int(micros * FLOPS_IN_MICRO), bytes_accessed=0, transcendentals=0
            ),
            compiler_params=pltpu.CompilerParams(vmem_limit_bytes=limit * MIB),
        )(*args, *after)

    return run


def tie(values, after):
    count = len(values)

    def nothing(*refs):
        pass

    return pl.pallas_call(
        nothing,
        out_shape=[jax.ShapeDtypeStruct(v.shape, v.dtype) for v in values],
        in_specs=[IN_ANY] * (count + len(after)),
        out_specs=[IN_ANY] * count,
        input_output_aliases={i: i for i in range(count)},
        compiler_params=pltpu.CompilerParams(vmem_limit_bytes=MIB),
    )(*values, *after)


def shape(*dims):
    return jax.ShapeDtypeStruct(dims, BF16)


FLAG = shape(16, 128)
FLOPS_IN_MICRO = 1.15e7


def shift(block, step, second):
    pairs = []
    for core in range(2):
        for y in range(SIDE):
            for x in range(SIDE):
                if (core == 0) != second:
                    target = y * SIDE + (x + step) % SIDE
                else:
                    target = (y + step) % SIDE * SIDE + x
                base = core * SIDE * SIDE
                pairs.append((base + y * SIDE + x, base + target))
    return lax.ppermute(block, ("dp", "tensor"), pairs)


def swap(block):
    return lax.ppermute(block, "dp", [(0, 1), (1, 0)])


def exchange(rows, parts):
    blocks = rows.reshape(parts, rows.shape[0] // parts, rows.shape[1])
    moved = lax.all_to_all(blocks, ("dp", "expert"), split_axis=0, concat_axis=0, tiled=True)
    return moved.reshape(rows.shape)


def spread(ids, gates, experts):
    tokens = ids.shape[1]
    dims = (experts * 2 * SLOTS, tokens)
    row = lax.broadcasted_iota(jnp.int32, dims, 0)
    expert, half, slot = row // (2 * SLOTS), row // SLOTS % 2, row % SLOTS
    first, second = ids[0:1, :] == expert, ids[1:2, :] == expert
    named = jnp.where(first | second, 1.0, 0.0).astype(F32)
    earlier = lax.broadcasted_iota(jnp.int32, (tokens, tokens), 0)
    later = lax.broadcasted_iota(jnp.int32, (tokens, tokens), 1)
    place = dot(named, jnp.where(earlier < later, 1.0, 0.0).astype(F32))
    select = jnp.where(place == slot.astype(F32), named, 0.0)
    weight = jnp.where(first, gates[0:1, :], 0.0) + jnp.where(second, gates[1:2, :], 0.0)
    weighted = select * weight
    return (
        [jnp.where(half == h, select, 0.0) for h in range(2)],
        [jnp.where(half == h, weighted, 0.0) for h in range(2)],
    )


def dispatch_kernel(experts, ids_ref, gates_ref, tokens_ref, cotangent_ref, opened, send_ref):
    select, weighted = spread(ids_ref[...], gates_ref[...].astype(F32), experts)
    width = tokens_ref.shape[1] // 2
    rows = experts * 2 * SLOTS
    for mats, ref, start in ((select, tokens_ref, 0), (weighted, cotangent_ref, rows)):
        total = dot(mats[0], ref[:, :width].astype(F32)) + dot(
            mats[1], ref[:, width:].astype(F32)
        )
        send_ref[start : start + rows, :] = total.astype(BF16)


def open_kernel(flag):
    flag[...] = jnp.zeros_like(flag)


def dispatch(experts, *args):
    rows = 4 * experts * SLOTS
    opened = call(open_kernel, FLAG, micros=1500)()
    return pl.pallas_call(
        functools.partial(dispatch_kernel, experts),
        out_shape=shape(rows, args[2].shape[1] // 2),
        in_specs=[IN_VMEM] * 4 + [IN_ANY],
        out_specs=IN_VMEM,
        compiler_params=pltpu.CompilerParams(vmem_limit_bytes=16 * MIB),
    )(*args, opened)


def combine_kernel(experts, ids_ref, gates_ref, home_ref, out_ref, back_ref):
    select, weighted = spread(ids_ref[...], gates_ref[...].astype(F32), experts)
    width = out_ref.shape[1] // 2
    rows = experts * 2 * SLOTS
    for mats, ref, start in ((weighted, out_ref, 0), (select, back_ref, rows)):
        part = home_ref[start : start + rows, :]
        for h in range(2):
            mat = mats[h].astype(BF16)
            ref[:, h * width : (h + 1) * width] = dot(mat, part, 0, 0).astype(BF16)


def half_matrix(rows, half, flip):
    dims = (2 * rows, rows) if flip else (rows, 2 * rows)
    plain = lax.broadcasted_iota(jnp.int32, dims, 1 if flip else 0)
    mixed = lax.broadcasted_iota(jnp.int32, dims, 0 if flip else 1)
    same = (mixed // (2 * SLOTS) == plain // SLOTS) & (mixed % SLOTS == plain % SLOTS)
    return jnp.where(same & (mixed // SLOTS % 2 == half), 1.0, 0.0).astype(BF16)


def unmix_kernel(mixed_ref, rows_ref):
    width = mixed_ref.shape[1]
    mixed = mixed_ref[...]
    for h in range(2):
        part = dot(half_matrix(rows_ref.shape[0], h, False), mixed)
        rows_ref[:, h * width : (h + 1) * width] = part.astype(BF16)


def load_kernel(*refs):
    for source, target in zip(refs[:3], refs[3:6]):
        target[...] = source[...]
    refs[6][...] = jnp.zeros_like(refs[6])


def join_kernel(top_ref, bottom_ref, rows_ref):
    rows = top_ref.shape[0]
    rows_ref[:rows, :] = top_ref[...]
    rows_ref[rows:, :] = bottom_ref[...]


def first_kernel(*refs):
    *pieces, gate_own, gate_far, up_own, up_far, down_own, down_far, act_ref = refs
    units = gate_own.shape[1]
    rows = pieces[0].shape[0]

    @pl.when(lax.axis_index("dp") == 0)
    def _():
        for i in range(0, len(pieces), 2):
            x = jnp.concatenate([p[...] for p in pieces[i : i + 2]], axis=0)
            at = slice(i * rows, (i + 2) * rows)
            for j, (gate, up) in enumerate(((gate_own, up_own), (gate_far, up_far))):
                gate_proj = dot(x, gate[...])
                up_proj = dot(x, up[...])
                sig = jax.nn.sigmoid(gate_proj)
                active = gate_proj * sig
                slope = up_proj * sig * (1.0 + gate_proj * (1.0 - sig))
                for k, value in enumerate((slope, active, active * up_proj)):
                    start = (2 * k + j) * units
                    act_ref[at, start : start + units] = value.astype(BF16)

    @pl.when(lax.axis_index("dp") != 0)
    def _():
        for i in range(0, len(pieces), 2):
            dy = jnp.concatenate([p[...] for p in pieces[i : i + 2]], axis=0)
            at = slice(i * rows, (i + 2) * rows)
            for j, down in enumerate((down_far, down_own)):
                value = dot(dy, down[...], 1, 1).astype(BF16)
                for k in range(2):
                    start = (2 * k + j) * units
                    act_ref[at, start : start + units] = value
                start = (4 + j) * units
                act_ref[at, start : start + units] = jnp.ones_like(value)


def block_of(refs, line, inner, rows):
    ref = refs[(0, 1, 1, 2)[line]]
    start = ((0, 0, 1, 0)[line] * SIDE + inner) * rows
    return ref[start : start + rows, :]


def line_product(mine, far, line, rows):
    return jnp.concatenate(
        [
            block_of(mine, line, inner, rows) * block_of(far, inner, line, rows)
            for inner in range(SIDE)
        ],
        axis=0,
    )


def second(product, weights, stores):
    gate_own, gate_far, up_own, up_far, down_own, down_far = weights
    units = gate_own.shape[1]
    width = down_own.shape[1]
    step = 512
    half = product.shape[0] // 2

    @pl.when(lax.axis_index("dp") == 0)
    def _():
        for c in range(0, width, step):
            total = dot(product[:, 4 * units : 5 * units], down_own[:, c : c + step]) + dot(
                product[:, 5 * units :], down_far[:, c : c + step]
            )
            for i, ref in enumerate(stores):
                ref[:, c : c + step] = total[i * half : (i + 1) * half].astype(BF16)

    @pl.when(lax.axis_index("dp") != 0)
    def _():
        for c in range(0, width, step):
            total = dot(product[:, :units], gate_far[c : c + step, :], 1, 1)
            for k, ref in enumerate((gate_own, up_far, up_own)):
                part = product[:, (k + 1) * units : (k + 2) * units]
                total = total + dot(part, ref[c : c + step, :], 1, 1)
            for i, ref in enumerate(stores):
                ref[:, c : c + step] = total[i * half : (i + 1) * half].astype(BF16)


def lines_kernel(rows, lines, *refs):
    mine, far, weights, stores, flag = refs[:3], refs[3:6], refs[6:12], refs[12:-1], refs[-1]
    flag[...] = jnp.zeros_like(flag)
    for i, line in enumerate(lines):
        product = line_product(mine, far, line, rows)
        second(product, weights, stores[2 * i : 2 * i + 2])


def own_line_kernel(rows, *refs):
    mine, far, weights, stores, act = refs[:3], refs[3:6], refs[6:12], refs[12:14], refs[14]
    for line in range(SIDE):
        product = line_product(mine, far, line, rows)
        act[line * SIDE * rows : (line + 1) * SIDE * rows, :] = product
        if line == 0:
            second(product, weights, stores)


STEP = 256


def column(pieces, at):
    return jnp.concatenate([p[:, at] for p in pieces], axis=0)


def columns_loop(width, body):
    def one(i, carry):
        body(pl.ds(pl.multiple_of(i * STEP, STEP), STEP))
        return carry

    lax.fori_loop(0, width // STEP, one, 0)


def far_grads_kernel(*refs):
    *pieces, act, send, send_more, flag = refs
    units = send.shape[1]
    flag[...] = jnp.zeros_like(flag)

    @pl.when(lax.axis_index("dp") == 0)
    def _():
        factor = jnp.concatenate(
            [act[:, units : 2 * units], act[:, 3 * units : 4 * units]], axis=1
        )

        def one(at):
            total = dot(column(pieces, at), factor, 0, 0).astype(BF16)
            send[at, :] = total[:, :units]
            send_more[at, :] = total[:, units:]

        columns_loop(send.shape[0], one)

    @pl.when(lax.axis_index("dp") != 0)
    def _():
        hidden = act[:, 4 * units : 5 * units].T

        def one(at):
            send[at, :] = dot(hidden, column(pieces, at)).astype(BF16)

        columns_loop(send.shape[0], one)


def own_grads_kernel(*refs):
    *pieces, act, got, got_more, gate_ref, up_ref, down_ref, flag = refs
    flag[...] = jnp.zeros_like(flag)
    units = gate_ref.shape[1]
    width = gate_ref.shape[0]

    @pl.when(lax.axis_index("dp") == 0)
    def _():
        factor = jnp.concatenate([act[:, :units], act[:, 2 * units : 3 * units]], axis=1)

        def one(at):
            total = dot(column(pieces, at), factor, 0, 0).astype(BF16)
            gate_ref[at, :] = total[:, :units]
            up_ref[at, :] = total[:, units:]
            down_ref[:, at] = got[at, :]

        columns_loop(width, one)

    @pl.when(lax.axis_index("dp") != 0)
    def _():
        hidden = act[:, 5 * units :].T

        def one(at):
            down_ref[:, at] = dot(hidden, column(pieces, at)).astype(BF16)
            gate_ref[at, :] = got[at, :]
            up_ref[at, :] = got_more[at, :]

        columns_loop(width, one)


def add(*parts):
    total = parts[0].astype(F32)
    for part in parts[1:]:
        total = total + part.astype(F32)
    return total.astype(BF16)


def relay_sum_kernel(low, low_got, high, high_got, low_sum, high_sum, flag):
    low_sum[...] = add(low[...], low_got[...])
    high_sum[...] = add(high[...], high_got[...])
    flag[...] = jnp.zeros_like(flag)


def line_sum_kernel(*refs):
    low, high, outs, flag = refs[:3], refs[3:6], refs[6:10], refs[10]
    flag[...] = jnp.zeros_like(flag)
    rows = outs[0].shape[0]
    for i, group in enumerate((low, high)):
        for j in range(2):
            at = slice(j * rows, (j + 1) * rows)
            outs[2 * i + j][...] = add(*[r[at, :] for r in group])


def home_kernel(own, one, two, three, mixed_ref):
    rows, width = own.shape
    total = add(own[...], one[...], two[...], three[...])
    low = dot(half_matrix(rows, 0, True), total[:, : width // 2])
    high = dot(half_matrix(rows, 1, True), total[:, width // 2 :])
    mixed_ref[...] = (low + high).astype(BF16)


def body(tokens, expert_ids, gate_values, cotangent, w_gate, w_up, w_down):
    tok_rows, width = tokens.shape
    experts = lax.axis_size("expert")
    sources = 2 * experts
    rows = sources * SLOTS
    units = w_gate.shape[2]
    ids, gates = expert_ids.T, gate_values.T

    shards = (w_gate[0], w_up[0], w_down[0])
    others = [swap(w) for w in shards]

    rows_out = dispatch(experts, ids, gates, tokens, cotangent)
    mixed = exchange(rows_out, sources)
    mine = call(unmix_kernel, shape(rows, width), after=others)(mixed)

    plus = shift(mine, -1, False)
    minus = shift(mine, 1, False)
    far = shift(mine, 2, False)
    *owns, loaded = call(
        load_kernel, tuple(shape(*w.shape) for w in shards) + (FLAG,), after=(mine,)
    )(*shards)
    weights = [w for pair in zip(owns, others) for w in pair]
    low = call(join_kernel, shape(2 * rows, width), after=(loaded,))(mine, plus)
    high = call(join_kernel, shape(2 * rows, width))(minus, far)
    low_minus = shift(low, 1, True)
    high_plus = shift(high, -1, True)
    high_minus = shift(high, 1, True)
    low_plus = shift(low, -1, True)

    def first(*pieces):
        count = len(pieces) * pieces[0].shape[0]
        return call(
            first_kernel, shape(count, 6 * units), micros=count / 128, limit=18
        )(*pieces, *weights)

    act_own = first(low, high)
    (low_minus,) = tie((low_minus,), (act_own,))
    low_far = shift(low_minus, 1, True)
    high_far = shift(high_plus, -1, True)
    line = SIDE * rows
    acts = [
        act_own,
        first(low_plus, high_plus, low_minus, high_minus),
        first(low_far, high_far),
    ]
    far_acts = [swap(a) for a in acts]
    pieces = (low, high, low_plus, high_plus, low_minus, high_minus, low_far, high_far)

    half = shape(line // 2, width)

    def lines(*which):
        return call(
            functools.partial(lines_kernel, rows, which),
            (half,) * (2 * len(which)) + (FLAG,),
            micros=1.5 * len(which),
            limit=18,
        )(*acts, *far_acts, *weights)

    out_low_far, out_high_far, _ = lines(3)
    low_got = shift(out_low_far, -1, True)
    high_got = shift(out_high_far, 1, True)
    out_low_plus, out_high_plus, out_low_minus, out_high_minus, sides = lines(1, 2)
    high_one = shift(out_high_minus, -1, True)
    low_one = shift(out_low_plus, 1, True)
    low_sum, high_sum, relayed = call(relay_sum_kernel, (half, half, FLAG))(
        out_low_minus, low_got, out_high_plus, high_got
    )
    low_two, high_two = shift(low_sum, -1, True), shift(high_sum, 1, True)
    out_low, out_high, act = call(
        functools.partial(own_line_kernel, rows),
        (half, half, shape(SIDE * line, 6 * units)),
        micros=1.5,
        limit=18,
        after=(sides,),
    )(*acts, *far_acts, *weights)

    column_shape, flat_shape = shape(width, units), shape(units, width)
    send, send_more, sent = call(
        far_grads_kernel,
        (column_shape, column_shape, FLAG),
        micros=8,
        limit=18,
        after=(relayed,),
    )(*pieces, act)
    got, got_more = swap(send), swap(send_more)

    block = shape(rows, width)
    own, plus_sum, minus_sum, far_sum, summed = call(
        line_sum_kernel, (block,) * 4 + (FLAG,), micros=1500, after=(sent,)
    )(out_low, low_one, low_two, out_high, high_one, high_two)
    got_plus = shift(plus_sum, 1, False)
    got_minus = shift(minus_sum, -1, False)
    got_far = shift(far_sum, 2, False)
    d_gate, d_up, d_down, settled = call(
        own_grads_kernel,
        (column_shape, column_shape, flat_shape, FLAG),
        micros=8,
        limit=18,
        after=(summed,),
    )(*pieces, act, got, got_more)
    back = call(home_kernel, shape(2 * rows, width // 2), after=(settled,))(
        own, got_plus, got_minus, got_far
    )
    home = exchange(back, sources)

    token_shape = shape(tok_rows, width)
    moe_out, d_tokens = call(
        functools.partial(combine_kernel, experts), (token_shape, token_shape)
    )(ids, gates, home)
    return moe_out, d_tokens, d_gate[None], d_up[None], d_down[None]


def solution(mesh):
    token_spec = P(("dp", "expert", "tensor"), None)
    column_spec = P("expert", None, ("dp", "tensor"))
    row_spec = P("expert", ("dp", "tensor"), None)
    in_specs = (token_spec,) * 4 + (column_spec, column_spec, row_spec)
    out_specs = (token_spec, token_spec, column_spec, column_spec, row_spec)
    return jax.shard_map(body, mesh=mesh, in_specs=in_specs, out_specs=out_specs, check_vma=False)
```

```python
import functools

import jax
import jax.numpy as jnp
from jax import lax
from jax.experimental import pallas as pl
from jax.experimental.pallas import tpu as pltpu
from jax.sharding import PartitionSpec as P

BF16 = jnp.bfloat16
F32 = jnp.float32
SIDE = 4
SLOTS = 4
MIB = 1024 * 1024
IN_VMEM = pl.BlockSpec(memory_space=pltpu.VMEM)
IN_ANY = pl.BlockSpec(memory_space=pl.ANY)


def dot(left, right, left_dim=1, right_dim=0):
    return lax.dot_general(
        left, right, (((left_dim,), (right_dim,)), ((), ())), preferred_element_type=F32
    )


def call(kernel, out_shape, micros=1, limit=16, after=()):
    def run(*args):
        specs = [IN_VMEM] * len(args)
        outs = jax.tree.map(lambda _: IN_VMEM, out_shape)
        count = len(args)

        def inner(*refs):
            kernel(*refs[:count], *refs[count + len(after) :])

        return pl.pallas_call(
            inner,
            out_shape=out_shape,
            in_specs=specs + [IN_ANY] * len(after),
            out_specs=outs,
            cost_estimate=pl.CostEstimate(
                flops=int(micros * FLOPS_IN_MICRO), bytes_accessed=0, transcendentals=0
            ),
            compiler_params=pltpu.CompilerParams(vmem_limit_bytes=limit * MIB),
        )(*args, *after)

    return run


def tie(values, after):
    count = len(values)

    def nothing(*refs):
        pass

    return pl.pallas_call(
        nothing,
        out_shape=[jax.ShapeDtypeStruct(v.shape, v.dtype) for v in values],
        in_specs=[IN_ANY] * (count + len(after)),
        out_specs=[IN_ANY] * count,
        input_output_aliases={i: i for i in range(count)},
        compiler_params=pltpu.CompilerParams(vmem_limit_bytes=MIB),
    )(*values, *after)


def shape(*dims):
    return jax.ShapeDtypeStruct(dims, BF16)


FLAG = shape(16, 128)
FLOPS_IN_MICRO = 1.15e7


def shift(block, step, second):
    pairs = []
    for core in range(2):
        for y in range(SIDE):
            for x in range(SIDE):
                if (core == 0) != second:
                    target = y * SIDE + (x + step) % SIDE
                else:
                    target = (y + step) % SIDE * SIDE + x
                base = core * SIDE * SIDE
                pairs.append((base + y * SIDE + x, base + target))
    return lax.ppermute(block, ("dp", "tensor"), pairs)


def swap(block):
    return lax.ppermute(block, "dp", [(0, 1), (1, 0)])


def exchange(rows, parts):
    blocks = rows.reshape(parts, rows.shape[0] // parts, rows.shape[1])
    moved = lax.all_to_all(blocks, ("dp", "expert"), split_axis=0, concat_axis=0, tiled=True)
    return moved.reshape(rows.shape)


def spread(ids, gates, experts):
    tokens = ids.shape[1]
    dims = (experts * 2 * SLOTS, tokens)
    row = lax.broadcasted_iota(jnp.int32, dims, 0)
    expert, half, slot = row // (2 * SLOTS), row // SLOTS % 2, row % SLOTS
    first, second = ids[0:1, :] == expert, ids[1:2, :] == expert
    named = jnp.where(first | second, 1.0, 0.0).astype(F32)
    earlier = lax.broadcasted_iota(jnp.int32, (tokens, tokens), 0)
    later = lax.broadcasted_iota(jnp.int32, (tokens, tokens), 1)
    place = dot(named, jnp.where(earlier < later, 1.0, 0.0).astype(F32))
    select = jnp.where(place == slot.astype(F32), named, 0.0)
    weight = jnp.where(first, gates[0:1, :], 0.0) + jnp.where(second, gates[1:2, :], 0.0)
    weighted = select * weight
    return (
        [jnp.where(half == h, select, 0.0) for h in range(2)],
        [jnp.where(half == h, weighted, 0.0) for h in range(2)],
    )


def dispatch_kernel(experts, ids_ref, gates_ref, tokens_ref, cotangent_ref, opened, send_ref):
    select, weighted = spread(ids_ref[...], gates_ref[...].astype(F32), experts)
    width = tokens_ref.shape[1] // 2
    rows = experts * 2 * SLOTS
    for mats, ref, start in ((select, tokens_ref, 0), (weighted, cotangent_ref, rows)):
        total = dot(mats[0], ref[:, :width].astype(F32)) + dot(
            mats[1], ref[:, width:].astype(F32)
        )
        send_ref[start : start + rows, :] = total.astype(BF16)


def open_kernel(flag):
    flag[...] = jnp.zeros_like(flag)


def dispatch(experts, *args):
    rows = 4 * experts * SLOTS
    opened = call(open_kernel, FLAG, micros=1500)()
    return pl.pallas_call(
        functools.partial(dispatch_kernel, experts),
        out_shape=shape(rows, args[2].shape[1] // 2),
        in_specs=[IN_VMEM] * 4 + [IN_ANY],
        out_specs=IN_VMEM,
        compiler_params=pltpu.CompilerParams(vmem_limit_bytes=16 * MIB),
    )(*args, opened)


def combine_kernel(experts, ids_ref, gates_ref, home_ref, out_ref, back_ref):
    select, weighted = spread(ids_ref[...], gates_ref[...].astype(F32), experts)
    width = out_ref.shape[1] // 2
    rows = experts * 2 * SLOTS
    for mats, ref, start in ((weighted, out_ref, 0), (select, back_ref, rows)):
        part = home_ref[start : start + rows, :]
        for h in range(2):
            mat = mats[h].astype(BF16)
            ref[:, h * width : (h + 1) * width] = dot(mat, part, 0, 0).astype(BF16)


def half_matrix(rows, half, flip):
    dims = (2 * rows, rows) if flip else (rows, 2 * rows)
    plain = lax.broadcasted_iota(jnp.int32, dims, 1 if flip else 0)
    mixed = lax.broadcasted_iota(jnp.int32, dims, 0 if flip else 1)
    same = (mixed // (2 * SLOTS) == plain // SLOTS) & (mixed % SLOTS == plain % SLOTS)
    return jnp.where(same & (mixed // SLOTS % 2 == half), 1.0, 0.0).astype(BF16)


def unmix_kernel(mixed_ref, rows_ref):
    width = mixed_ref.shape[1]
    mixed = mixed_ref[...]
    for h in range(2):
        part = dot(half_matrix(rows_ref.shape[0], h, False), mixed)
        rows_ref[:, h * width : (h + 1) * width] = part.astype(BF16)


def load_kernel(*refs):
    for source, target in zip(refs[:3], refs[3:6]):
        target[...] = source[...]
    refs[6][...] = jnp.zeros_like(refs[6])


def join_kernel(top_ref, bottom_ref, rows_ref):
    rows = top_ref.shape[0]
    rows_ref[:rows, :] = top_ref[...]
    rows_ref[rows:, :] = bottom_ref[...]


def first_kernel(*refs):
    *pieces, gate_own, gate_far, up_own, up_far, down_own, down_far, act_ref = refs
    units = gate_own.shape[1]
    rows = pieces[0].shape[0]

    @pl.when(lax.axis_index("dp") == 0)
    def _():
        for i in range(0, len(pieces), 2):
            x = jnp.concatenate([p[...] for p in pieces[i : i + 2]], axis=0)
            at = slice(i * rows, (i + 2) * rows)
            for j, (gate, up) in enumerate(((gate_own, up_own), (gate_far, up_far))):
                gate_proj = dot(x, gate[...])
                up_proj = dot(x, up[...])
                sig = jax.nn.sigmoid(gate_proj)
                active = gate_proj * sig
                slope = up_proj * sig * (1.0 + gate_proj * (1.0 - sig))
                for k, value in enumerate((slope, active, active * up_proj)):
                    start = (2 * k + j) * units
                    act_ref[at, start : start + units] = value.astype(BF16)

    @pl.when(lax.axis_index("dp") != 0)
    def _():
        for i in range(0, len(pieces), 2):
            dy = jnp.concatenate([p[...] for p in pieces[i : i + 2]], axis=0)
            at = slice(i * rows, (i + 2) * rows)
            for j, down in enumerate((down_far, down_own)):
                value = dot(dy, down[...], 1, 1).astype(BF16)
                for k in range(2):
                    start = (2 * k + j) * units
                    act_ref[at, start : start + units] = value
                start = (4 + j) * units
                act_ref[at, start : start + units] = jnp.ones_like(value)


def block_of(refs, line, inner, rows):
    ref = refs[(0, 1, 1, 2)[line]]
    start = ((0, 0, 1, 0)[line] * SIDE + inner) * rows
    return ref[start : start + rows, :]


def line_product(mine, far, line, rows):
    return jnp.concatenate(
        [
            block_of(mine, line, inner, rows) * block_of(far, inner, line, rows)
            for inner in range(SIDE)
        ],
        axis=0,
    )


def second(product, weights, stores):
    gate_own, gate_far, up_own, up_far, down_own, down_far = weights
    units = gate_own.shape[1]
    width = down_own.shape[1]
    step = 512
    half = product.shape[0] // 2

    @pl.when(lax.axis_index("dp") == 0)
    def _():
        for c in range(0, width, step):
            total = dot(product[:, 4 * units : 5 * units], down_own[:, c : c + step]) + dot(
                product[:, 5 * units :], down_far[:, c : c + step]
            )
            for i, ref in enumerate(stores):
                ref[:, c : c + step] = total[i * half : (i + 1) * half].astype(BF16)

    @pl.when(lax.axis_index("dp") != 0)
    def _():
        for c in range(0, width, step):
            total = dot(product[:, :units], gate_far[c : c + step, :], 1, 1)
            for k, ref in enumerate((gate_own, up_far, up_own)):
                part = product[:, (k + 1) * units : (k + 2) * units]
                total = total + dot(part, ref[c : c + step, :], 1, 1)
            for i, ref in enumerate(stores):
                ref[:, c : c + step] = total[i * half : (i + 1) * half].astype(BF16)


def lines_kernel(rows, lines, *refs):
    mine, far, weights, stores, flag = refs[:3], refs[3:6], refs[6:12], refs[12:-1], refs[-1]
    flag[...] = jnp.zeros_like(flag)
    for i, line in enumerate(lines):
        product = line_product(mine, far, line, rows)
        second(product, weights, stores[2 * i : 2 * i + 2])


def own_line_kernel(rows, *refs):
    mine, far, weights, stores, act = refs[:3], refs[3:6], refs[6:12], refs[12:14], refs[14]
    for line in range(SIDE):
        product = line_product(mine, far, line, rows)
        act[line * SIDE * rows : (line + 1) * SIDE * rows, :] = product
        if line == 0:
            second(product, weights, stores)


STEP = 256


def column(pieces, at):
    return jnp.concatenate([p[:, at] for p in pieces], axis=0)


def columns_loop(width, body):
    def one(i, carry):
        body(pl.ds(pl.multiple_of(i * STEP, STEP), STEP))
        return carry

    lax.fori_loop(0, width // STEP, one, 0)


def far_grads_kernel(*refs):
    *pieces, act, send, send_more, flag = refs
    units = send.shape[1]
    flag[...] = jnp.zeros_like(flag)

    @pl.when(lax.axis_index("dp") == 0)
    def _():
        factor = jnp.concatenate(
            [act[:, units : 2 * units], act[:, 3 * units : 4 * units]], axis=1
        )

        def one(at):
            total = dot(column(pieces, at), factor, 0, 0).astype(BF16)
            send[at, :] = total[:, :units]
            send_more[at, :] = total[:, units:]

        columns_loop(send.shape[0], one)

    @pl.when(lax.axis_index("dp") != 0)
    def _():
        hidden = act[:, 4 * units : 5 * units].T

        def one(at):
            send[at, :] = dot(hidden, column(pieces, at)).astype(BF16)

        columns_loop(send.shape[0], one)


def own_grads_kernel(*refs):
    *pieces, act, got, got_more, gate_ref, up_ref, down_ref, flag = refs
    flag[...] = jnp.zeros_like(flag)
    units = gate_ref.shape[1]
    width = gate_ref.shape[0]

    @pl.when(lax.axis_index("dp") == 0)
    def _():
        factor = jnp.concatenate([act[:, :units], act[:, 2 * units : 3 * units]], axis=1)

        def one(at):
            total = dot(column(pieces, at), factor, 0, 0).astype(BF16)
            gate_ref[at, :] = total[:, :units]
            up_ref[at, :] = total[:, units:]
            down_ref[:, at] = got[at, :]

        columns_loop(width, one)

    @pl.when(lax.axis_index("dp") != 0)
    def _():
        hidden = act[:, 5 * units :].T

        def one(at):
            down_ref[:, at] = dot(hidden, column(pieces, at)).astype(BF16)
            gate_ref[at, :] = got[at, :]
            up_ref[at, :] = got_more[at, :]

        columns_loop(width, one)


def add(*parts):
    total = parts[0].astype(F32)
    for part in parts[1:]:
        total = total + part.astype(F32)
    return total.astype(BF16)


def relay_sum_kernel(own, got, total, flag):
    total[...] = add(own[...], got[...])
    flag[...] = jnp.zeros_like(flag)


def line_sum_kernel(*refs):
    low, high, outs, flag = refs[:3], refs[3:6], refs[6:10], refs[10]
    flag[...] = jnp.zeros_like(flag)
    rows = outs[0].shape[0]
    for i, group in enumerate((low, high)):
        for j in range(2):
            at = slice(j * rows, (j + 1) * rows)
            outs[2 * i + j][...] = add(*[r[at, :] for r in group])


def home_kernel(own, one, two, three, mixed_ref):
    rows, width = own.shape
    total = add(own[...], one[...], two[...], three[...])
    low = dot(half_matrix(rows, 0, True), total[:, : width // 2])
    high = dot(half_matrix(rows, 1, True), total[:, width // 2 :])
    mixed_ref[...] = (low + high).astype(BF16)


def body(tokens, expert_ids, gate_values, cotangent, w_gate, w_up, w_down):
    tok_rows, width = tokens.shape
    experts = lax.axis_size("expert")
    sources = 2 * experts
    rows = sources * SLOTS
    units = w_gate.shape[2]
    ids, gates = expert_ids.T, gate_values.T

    shards = (w_gate[0], w_up[0], w_down[0])
    others = [swap(w) for w in shards]

    rows_out = dispatch(experts, ids, gates, tokens, cotangent)
    mixed = exchange(rows_out, sources)
    mine = call(unmix_kernel, shape(rows, width), after=others)(mixed)

    plus = shift(mine, -1, False)
    minus = shift(mine, 1, False)
    far = shift(mine, 2, False)
    *owns, loaded = call(
        load_kernel, tuple(shape(*w.shape) for w in shards) + (FLAG,), after=(mine,)
    )(*shards)
    weights = [w for pair in zip(owns, others) for w in pair]
    low = call(join_kernel, shape(2 * rows, width), after=(loaded,))(mine, plus)
    high = call(join_kernel, shape(2 * rows, width))(minus, far)
    low_minus = shift(low, 1, True)
    high_plus = shift(high, -1, True)
    high_minus = shift(high, 1, True)
    low_plus = shift(low, -1, True)

    def first(*pieces):
        count = len(pieces) * pieces[0].shape[0]
        return call(
            first_kernel, shape(count, 6 * units), micros=count / 128, limit=18
        )(*pieces, *weights)

    act_own = first(low, high)
    (low_minus,) = tie((low_minus,), (act_own,))
    low_far = shift(low_minus, 1, True)
    high_far = shift(high_plus, -1, True)
    line = SIDE * rows
    acts = [
        act_own,
        first(low_plus, high_plus, low_minus, high_minus),
        first(low_far, high_far),
    ]
    far_acts = [swap(a) for a in acts]
    pieces = (low, high, low_plus, high_plus, low_minus, high_minus, low_far, high_far)

    half = shape(line // 2, width)

    def lines(*which):
        return call(
            functools.partial(lines_kernel, rows, which),
            (half,) * (2 * len(which)) + (FLAG,),
            micros=1.5 * len(which),
            limit=18,
        )(*acts, *far_acts, *weights)

    out_low_far, out_high_far, _ = lines(3)
    low_got = shift(out_low_far, -1, True)
    high_got = shift(out_high_far, 1, True)
    out_low_plus, out_high_plus, out_low_minus, out_high_minus, sides = lines(1, 2)
    high_one = shift(out_high_minus, -1, True)
    low_one = shift(out_low_plus, 1, True)
    relay_sum = call(relay_sum_kernel, (half, FLAG))
    low_sum, low_relayed = relay_sum(out_low_minus, low_got)
    low_two = shift(low_sum, -1, True)
    high_sum, high_relayed = relay_sum(out_high_plus, high_got)
    high_two = shift(high_sum, 1, True)
    out_low, out_high, act = call(
        functools.partial(own_line_kernel, rows),
        (half, half, shape(SIDE * line, 6 * units)),
        micros=1.5,
        limit=18,
        after=(sides,),
    )(*acts, *far_acts, *weights)

    column_shape, flat_shape = shape(width, units), shape(units, width)
    send, send_more, sent = call(
        far_grads_kernel,
        (column_shape, column_shape, FLAG),
        micros=8,
        limit=18,
        after=(low_relayed, high_relayed),
    )(*pieces, act)
    got, got_more = swap(send), swap(send_more)

    block = shape(rows, width)
    own, plus_sum, minus_sum, far_sum, summed = call(
        line_sum_kernel, (block,) * 4 + (FLAG,), micros=1500, after=(sent,)
    )(out_low, low_one, low_two, out_high, high_one, high_two)
    got_plus = shift(plus_sum, 1, False)
    got_minus = shift(minus_sum, -1, False)
    got_far = shift(far_sum, 2, False)
    d_gate, d_up, d_down, settled = call(
        own_grads_kernel,
        (column_shape, column_shape, flat_shape, FLAG),
        micros=8,
        limit=18,
        after=(summed,),
    )(*pieces, act, got, got_more)
    back = call(home_kernel, shape(2 * rows, width // 2), after=(settled,))(
        own, got_plus, got_minus, got_far
    )
    home = exchange(back, sources)

    token_shape = shape(tok_rows, width)
    moe_out, d_tokens = call(
        functools.partial(combine_kernel, experts), (token_shape, token_shape)
    )(ids, gates, home)
    return moe_out, d_tokens, d_gate[None], d_up[None], d_down[None]


def solution(mesh):
    token_spec = P(("dp", "expert", "tensor"), None)
    column_spec = P("expert", None, ("dp", "tensor"))
    row_spec = P("expert", ("dp", "tensor"), None)
    in_specs = (token_spec,) * 4 + (column_spec, column_spec, row_spec)
    out_specs = (token_spec, token_spec, column_spec, column_spec, row_spec)
    return jax.shard_map(body, mesh=mesh, in_specs=in_specs, out_specs=out_specs, check_vma=False)
```

```python
import functools

import jax
import jax.numpy as jnp
from jax import lax
from jax.experimental import pallas as pl
from jax.experimental.pallas import tpu as pltpu
from jax.sharding import PartitionSpec as P

BF16 = jnp.bfloat16
F32 = jnp.float32
SIDE = 4
SLOTS = 4
MIB = 1024 * 1024
IN_VMEM = pl.BlockSpec(memory_space=pltpu.VMEM)
IN_ANY = pl.BlockSpec(memory_space=pl.ANY)


def dot(left, right, left_dim=1, right_dim=0):
    return lax.dot_general(
        left, right, (((left_dim,), (right_dim,)), ((), ())), preferred_element_type=F32
    )


def call(kernel, out_shape, micros=1, limit=16, after=()):
    def run(*args):
        specs = [IN_VMEM] * len(args)
        outs = jax.tree.map(lambda _: IN_VMEM, out_shape)
        count = len(args)

        def inner(*refs):
            kernel(*refs[:count], *refs[count + len(after) :])

        return pl.pallas_call(
            inner,
            out_shape=out_shape,
            in_specs=specs + [IN_ANY] * len(after),
            out_specs=outs,
            cost_estimate=pl.CostEstimate(
                flops=int(micros * FLOPS_IN_MICRO), bytes_accessed=0, transcendentals=0
            ),
            compiler_params=pltpu.CompilerParams(vmem_limit_bytes=limit * MIB),
        )(*args, *after)

    return run


def tie(values, after):
    count = len(values)

    def nothing(*refs):
        pass

    return pl.pallas_call(
        nothing,
        out_shape=[jax.ShapeDtypeStruct(v.shape, v.dtype) for v in values],
        in_specs=[IN_ANY] * (count + len(after)),
        out_specs=[IN_ANY] * count,
        input_output_aliases={i: i for i in range(count)},
        compiler_params=pltpu.CompilerParams(vmem_limit_bytes=MIB),
    )(*values, *after)


def shape(*dims):
    return jax.ShapeDtypeStruct(dims, BF16)


FLAG = shape(16, 128)
FLOPS_IN_MICRO = 1.15e7


def shift(block, step, second):
    pairs = []
    for core in range(2):
        for y in range(SIDE):
            for x in range(SIDE):
                if (core == 0) != second:
                    target = y * SIDE + (x + step) % SIDE
                else:
                    target = (y + step) % SIDE * SIDE + x
                base = core * SIDE * SIDE
                pairs.append((base + y * SIDE + x, base + target))
    return lax.ppermute(block, ("dp", "tensor"), pairs)


def swap(block):
    return lax.ppermute(block, "dp", [(0, 1), (1, 0)])


def exchange(rows, parts):
    blocks = rows.reshape(parts, rows.shape[0] // parts, rows.shape[1])
    moved = lax.all_to_all(blocks, ("dp", "expert"), split_axis=0, concat_axis=0, tiled=True)
    return moved.reshape(rows.shape)


def spread(ids, gates, experts):
    tokens = ids.shape[1]
    dims = (experts * 2 * SLOTS, tokens)
    row = lax.broadcasted_iota(jnp.int32, dims, 0)
    expert, half, slot = row // (2 * SLOTS), row // SLOTS % 2, row % SLOTS
    first, second = ids[0:1, :] == expert, ids[1:2, :] == expert
    named = jnp.where(first | second, 1.0, 0.0).astype(F32)
    earlier = lax.broadcasted_iota(jnp.int32, (tokens, tokens), 0)
    later = lax.broadcasted_iota(jnp.int32, (tokens, tokens), 1)
    place = dot(named, jnp.where(earlier < later, 1.0, 0.0).astype(F32))
    select = jnp.where(place == slot.astype(F32), named, 0.0)
    weight = jnp.where(first, gates[0:1, :], 0.0) + jnp.where(second, gates[1:2, :], 0.0)
    weighted = select * weight
    return (
        [jnp.where(half == h, select, 0.0) for h in range(2)],
        [jnp.where(half == h, weighted, 0.0) for h in range(2)],
    )


def dispatch_kernel(experts, ids_ref, gates_ref, tokens_ref, cotangent_ref, opened, send_ref):
    select, weighted = spread(ids_ref[...], gates_ref[...].astype(F32), experts)
    width = tokens_ref.shape[1] // 2
    rows = experts * 2 * SLOTS
    for mats, ref, start in ((select, tokens_ref, 0), (weighted, cotangent_ref, rows)):
        total = dot(mats[0], ref[:, :width].astype(F32)) + dot(
            mats[1], ref[:, width:].astype(F32)
        )
        send_ref[start : start + rows, :] = total.astype(BF16)


def open_kernel(flag):
    flag[...] = jnp.zeros_like(flag)


def dispatch(experts, *args):
    rows = 4 * experts * SLOTS
    opened = call(open_kernel, FLAG, micros=1500)()
    return pl.pallas_call(
        functools.partial(dispatch_kernel, experts),
        out_shape=shape(rows, args[2].shape[1] // 2),
        in_specs=[IN_VMEM] * 4 + [IN_ANY],
        out_specs=IN_VMEM,
        compiler_params=pltpu.CompilerParams(vmem_limit_bytes=16 * MIB),
    )(*args, opened)


def combine_kernel(experts, ids_ref, gates_ref, home_ref, out_ref, back_ref):
    select, weighted = spread(ids_ref[...], gates_ref[...].astype(F32), experts)
    width = out_ref.shape[1] // 2
    rows = experts * 2 * SLOTS
    for mats, ref, start in ((weighted, out_ref, 0), (select, back_ref, rows)):
        part = home_ref[start : start + rows, :]
        for h in range(2):
            mat = mats[h].astype(BF16)
            ref[:, h * width : (h + 1) * width] = dot(mat, part, 0, 0).astype(BF16)


def half_matrix(rows, half, flip):
    dims = (2 * rows, rows) if flip else (rows, 2 * rows)
    plain = lax.broadcasted_iota(jnp.int32, dims, 1 if flip else 0)
    mixed = lax.broadcasted_iota(jnp.int32, dims, 0 if flip else 1)
    same = (mixed // (2 * SLOTS) == plain // SLOTS) & (mixed % SLOTS == plain % SLOTS)
    return jnp.where(same & (mixed // SLOTS % 2 == half), 1.0, 0.0).astype(BF16)


def unmix_kernel(mixed_ref, rows_ref):
    width = mixed_ref.shape[1]
    mixed = mixed_ref[...]
    for h in range(2):
        part = dot(half_matrix(rows_ref.shape[0], h, False), mixed)
        rows_ref[:, h * width : (h + 1) * width] = part.astype(BF16)


def load_kernel(*refs):
    for source, target in zip(refs[:3], refs[3:6]):
        target[...] = source[...]
    refs[6][...] = jnp.zeros_like(refs[6])


def join_kernel(top_ref, bottom_ref, rows_ref):
    rows = top_ref.shape[0]
    rows_ref[:rows, :] = top_ref[...]
    rows_ref[rows:, :] = bottom_ref[...]


def first_kernel(*refs):
    *pieces, gate_own, gate_far, up_own, up_far, down_own, down_far, act_ref = refs
    units = gate_own.shape[1]
    rows = pieces[0].shape[0]

    @pl.when(lax.axis_index("dp") == 0)
    def _():
        for i in range(0, len(pieces), 2):
            x = jnp.concatenate([p[...] for p in pieces[i : i + 2]], axis=0)
            at = slice(i * rows, (i + 2) * rows)
            for j, (gate, up) in enumerate(((gate_own, up_own), (gate_far, up_far))):
                gate_proj = dot(x, gate[...])
                up_proj = dot(x, up[...])
                sig = jax.nn.sigmoid(gate_proj)
                active = gate_proj * sig
                slope = up_proj * sig * (1.0 + gate_proj * (1.0 - sig))
                for k, value in enumerate((slope, active, active * up_proj)):
                    start = (2 * k + j) * units
                    act_ref[at, start : start + units] = value.astype(BF16)

    @pl.when(lax.axis_index("dp") != 0)
    def _():
        for i in range(0, len(pieces), 2):
            dy = jnp.concatenate([p[...] for p in pieces[i : i + 2]], axis=0)
            at = slice(i * rows, (i + 2) * rows)
            for j, down in enumerate((down_far, down_own)):
                value = dot(dy, down[...], 1, 1).astype(BF16)
                for k in range(2):
                    start = (2 * k + j) * units
                    act_ref[at, start : start + units] = value
                start = (4 + j) * units
                act_ref[at, start : start + units] = jnp.ones_like(value)


def block_of(refs, line, inner, rows):
    ref = refs[(0, 1, 1, 2)[line]]
    start = ((0, 0, 1, 0)[line] * SIDE + inner) * rows
    return ref[start : start + rows, :]


def line_product(mine, far, line, rows):
    return jnp.concatenate(
        [
            block_of(mine, line, inner, rows) * block_of(far, inner, line, rows)
            for inner in range(SIDE)
        ],
        axis=0,
    )


def second(product, weights, stores):
    gate_own, gate_far, up_own, up_far, down_own, down_far = weights
    units = gate_own.shape[1]
    width = down_own.shape[1]
    step = 512
    starts = [0]
    for ref in stores:
        starts.append(starts[-1] + ref.shape[0])

    @pl.when(lax.axis_index("dp") == 0)
    def _():
        for c in range(0, width, step):
            total = dot(product[:, 4 * units : 5 * units], down_own[:, c : c + step]) + dot(
                product[:, 5 * units :], down_far[:, c : c + step]
            )
            for i, ref in enumerate(stores):
                ref[:, c : c + step] = total[starts[i] : starts[i + 1]].astype(BF16)

    @pl.when(lax.axis_index("dp") != 0)
    def _():
        for c in range(0, width, step):
            total = dot(product[:, :units], gate_far[c : c + step, :], 1, 1)
            for k, ref in enumerate((gate_own, up_far, up_own)):
                part = product[:, (k + 1) * units : (k + 2) * units]
                total = total + dot(part, ref[c : c + step, :], 1, 1)
            for i, ref in enumerate(stores):
                ref[:, c : c + step] = total[starts[i] : starts[i + 1]].astype(BF16)


def far_early_kernel(rows, mine, own_far, side_far, *refs):
    weights, low_store, two_store = refs[:6], refs[6], refs[7]
    far = (own_far, side_far)
    product = jnp.concatenate(
        [mine[i * rows : (i + 1) * rows, :] * block_of(far, i, 3, rows) for i in range(3)], axis=0
    )
    second(product, weights, (low_store, two_store))


def far_last_kernel(rows, mine, far, *refs):
    weights, store, flag = refs[:6], refs[6], refs[7]
    flag[...] = jnp.zeros_like(flag)
    second(mine[3 * rows :, :] * far[3 * rows :, :], weights, (store,))


def lines_kernel(rows, lines, *refs):
    mine, far, weights, stores, flag = refs[:3], refs[3:6], refs[6:12], refs[12:-1], refs[-1]
    flag[...] = jnp.zeros_like(flag)
    for i, line in enumerate(lines):
        product = line_product(mine, far, line, rows)
        second(product, weights, stores[2 * i : 2 * i + 2])


def own_line_kernel(rows, *refs):
    mine, far, weights, stores, act = refs[:3], refs[3:6], refs[6:12], refs[12:14], refs[14]
    for line in range(SIDE):
        product = line_product(mine, far, line, rows)
        act[line * SIDE * rows : (line + 1) * SIDE * rows, :] = product
        if line == 0:
            second(product, weights, stores)


STEP = 256


def column(pieces, at):
    return jnp.concatenate([p[:, at] for p in pieces], axis=0)


def columns_loop(width, body):
    def one(i, carry):
        body(pl.ds(pl.multiple_of(i * STEP, STEP), STEP))
        return carry

    lax.fori_loop(0, width // STEP, one, 0)


def far_grads_kernel(*refs):
    *pieces, act, send, send_more, flag = refs
    units = send.shape[1]
    flag[...] = jnp.zeros_like(flag)

    @pl.when(lax.axis_index("dp") == 0)
    def _():
        factor = jnp.concatenate(
            [act[:, units : 2 * units], act[:, 3 * units : 4 * units]], axis=1
        )

        def one(at):
            total = dot(column(pieces, at), factor, 0, 0).astype(BF16)
            send[at, :] = total[:, :units]
            send_more[at, :] = total[:, units:]

        columns_loop(send.shape[0], one)

    @pl.when(lax.axis_index("dp") != 0)
    def _():
        hidden = act[:, 4 * units : 5 * units].T

        def one(at):
            send[at, :] = dot(hidden, column(pieces, at)).astype(BF16)

        columns_loop(send.shape[0], one)


def own_grads_kernel(*refs):
    *pieces, act, got, got_more, gate_ref, up_ref, down_ref, flag = refs
    flag[...] = jnp.zeros_like(flag)
    units = gate_ref.shape[1]
    width = gate_ref.shape[0]

    @pl.when(lax.axis_index("dp") == 0)
    def _():
        factor = jnp.concatenate([act[:, :units], act[:, 2 * units : 3 * units]], axis=1)

        def one(at):
            total = dot(column(pieces, at), factor, 0, 0).astype(BF16)
            gate_ref[at, :] = total[:, :units]
            up_ref[at, :] = total[:, units:]
            down_ref[:, at] = got[at, :]

        columns_loop(width, one)

    @pl.when(lax.axis_index("dp") != 0)
    def _():
        hidden = act[:, 5 * units :].T

        def one(at):
            down_ref[:, at] = dot(hidden, column(pieces, at)).astype(BF16)
            gate_ref[at, :] = got[at, :]
            up_ref[at, :] = got_more[at, :]

        columns_loop(width, one)


def add(*parts):
    total = parts[0].astype(F32)
    for part in parts[1:]:
        total = total + part.astype(F32)
    return total.astype(BF16)


def relay_sum_kernel(own, *refs):
    got, total, flag = refs[:-2], refs[-2], refs[-1]
    rows = got[0].shape[0]
    for i, ref in enumerate(got):
        at = slice(i * rows, (i + 1) * rows)
        total[at, :] = add(own[at, :], ref[...])
    flag[...] = jnp.zeros_like(flag)


def line_sum_kernel(*refs):
    low, high, outs, flag = refs[:3], refs[3:6], refs[6:10], refs[10]
    flag[...] = jnp.zeros_like(flag)
    rows = outs[0].shape[0]
    for i, group in enumerate((low, high)):
        for j in range(2):
            at = slice(j * rows, (j + 1) * rows)
            outs[2 * i + j][...] = add(*[r[at, :] for r in group])


def home_kernel(own, one, two, three, mixed_ref):
    rows, width = own.shape
    total = add(own[...], one[...], two[...], three[...])
    low = dot(half_matrix(rows, 0, True), total[:, : width // 2])
    high = dot(half_matrix(rows, 1, True), total[:, width // 2 :])
    mixed_ref[...] = (low + high).astype(BF16)


def body(tokens, expert_ids, gate_values, cotangent, w_gate, w_up, w_down):
    tok_rows, width = tokens.shape
    experts = lax.axis_size("expert")
    sources = 2 * experts
    rows = sources * SLOTS
    units = w_gate.shape[2]
    ids, gates = expert_ids.T, gate_values.T

    shards = (w_gate[0], w_up[0], w_down[0])
    others = [swap(w) for w in shards]

    rows_out = dispatch(experts, ids, gates, tokens, cotangent)
    mixed = exchange(rows_out, sources)
    mine = call(unmix_kernel, shape(rows, width), after=others)(mixed)

    plus = shift(mine, -1, False)
    minus = shift(mine, 1, False)
    far = shift(mine, 2, False)
    *owns, loaded = call(
        load_kernel, tuple(shape(*w.shape) for w in shards) + (FLAG,), after=(mine,)
    )(*shards)
    weights = [w for pair in zip(owns, others) for w in pair]
    low = call(join_kernel, shape(2 * rows, width), after=(loaded,))(mine, plus)
    high = call(join_kernel, shape(2 * rows, width))(minus, far)
    low_minus = shift(low, 1, True)
    high_plus = shift(high, -1, True)
    high_minus = shift(high, 1, True)
    low_plus = shift(low, -1, True)

    def first(*pieces, micros=2):
        count = len(pieces) * pieces[0].shape[0]
        return call(
            first_kernel, shape(count, 6 * units), micros=micros, limit=18
        )(*pieces, *weights)

    act_own = first(low, high)
    (low_minus,) = tie((low_minus,), (act_own,))
    low_far = shift(low_minus, 1, True)
    high_far = shift(high_plus, -1, True)
    line = SIDE * rows
    acts = [
        act_own,
        first(low_plus, high_plus, low_minus, high_minus),
        first(low_far, high_far, micros=1000),
    ]
    far_acts = [swap(a) for a in acts]
    pieces = (low, high, low_plus, high_plus, low_minus, high_minus, low_far, high_far)

    half = shape(line // 2, width)

    block = shape(rows, width)
    out_low_far, out_far_two = call(
        functools.partial(far_early_kernel, rows), (half, block), limit=18
    )(acts[2], far_acts[0], far_acts[1], *weights)
    low_got = shift(out_low_far, -1, True)
    two_got = shift(out_far_two, 1, True)
    out_far_three, last = call(
        functools.partial(far_last_kernel, rows), (block, FLAG), limit=18
    )(acts[2], far_acts[2], *weights)
    three_got = shift(out_far_three, 1, True)
    def lines(*which):
        return call(
            functools.partial(lines_kernel, rows, which),
            (half,) * (2 * len(which)) + (FLAG,),
            micros=1.5 * len(which),
            limit=18,
            after=(last,),
        )(*acts, *far_acts, *weights)

    out_low_plus, out_high_plus, out_low_minus, out_high_minus, sides = lines(1, 2)
    high_one = shift(out_high_minus, -1, True)
    low_one = shift(out_low_plus, 1, True)
    relay_sum = call(relay_sum_kernel, (half, FLAG))
    low_sum, low_relayed = relay_sum(out_low_minus, low_got)
    low_two = shift(low_sum, -1, True)
    high_sum, high_relayed = relay_sum(out_high_plus, two_got, three_got)
    high_two = shift(high_sum, 1, True)
    out_low, out_high, act = call(
        functools.partial(own_line_kernel, rows),
        (half, half, shape(SIDE * line, 6 * units)),
        micros=1.5,
        limit=18,
        after=(sides,),
    )(*acts, *far_acts, *weights)

    column_shape, flat_shape = shape(width, units), shape(units, width)
    send, send_more, sent = call(
        far_grads_kernel,
        (column_shape, column_shape, FLAG),
        micros=8,
        limit=18,
        after=(low_relayed, high_relayed),
    )(*pieces, act)
    got, got_more = swap(send), swap(send_more)

    block = shape(rows, width)
    own, plus_sum, minus_sum, far_sum, summed = call(
        line_sum_kernel, (block,) * 4 + (FLAG,), micros=1500, after=(sent,)
    )(out_low, low_one, low_two, out_high, high_one, high_two)
    got_plus = shift(plus_sum, 1, False)
    got_minus = shift(minus_sum, -1, False)
    got_far = shift(far_sum, 2, False)
    d_gate, d_up, d_down, settled = call(
        own_grads_kernel,
        (column_shape, column_shape, flat_shape, FLAG),
        micros=8,
        limit=18,
        after=(summed,),
    )(*pieces, act, got, got_more)
    back = call(home_kernel, shape(2 * rows, width // 2), after=(settled,))(
        own, got_plus, got_minus, got_far
    )
    home = exchange(back, sources)

    token_shape = shape(tok_rows, width)
    moe_out, d_tokens = call(
        functools.partial(combine_kernel, experts), (token_shape, token_shape)
    )(ids, gates, home)
    return moe_out, d_tokens, d_gate[None], d_up[None], d_down[None]


def solution(mesh):
    token_spec = P(("dp", "expert", "tensor"), None)
    column_spec = P("expert", None, ("dp", "tensor"))
    row_spec = P("expert", ("dp", "tensor"), None)
    in_specs = (token_spec,) * 4 + (column_spec, column_spec, row_spec)
    out_specs = (token_spec, token_spec, column_spec, column_spec, row_spec)
    return jax.shard_map(body, mesh=mesh, in_specs=in_specs, out_specs=out_specs, check_vma=False)
```

```python
import functools

import jax
import jax.numpy as jnp
from jax import lax
from jax.experimental import pallas as pl
from jax.experimental.pallas import tpu as pltpu
from jax.sharding import PartitionSpec as P

BF16 = jnp.bfloat16
F32 = jnp.float32
SIDE = 4
SLOTS = 4
MIB = 1024 * 1024
IN_VMEM = pl.BlockSpec(memory_space=pltpu.VMEM)
IN_ANY = pl.BlockSpec(memory_space=pl.ANY)


def dot(left, right, left_dim=1, right_dim=0):
    return lax.dot_general(
        left, right, (((left_dim,), (right_dim,)), ((), ())), preferred_element_type=F32
    )


def call(kernel, out_shape, micros=1, limit=16, after=()):
    def run(*args):
        specs = [IN_VMEM] * len(args)
        outs = jax.tree.map(lambda _: IN_VMEM, out_shape)
        count = len(args)

        def inner(*refs):
            kernel(*refs[:count], *refs[count + len(after) :])

        return pl.pallas_call(
            inner,
            out_shape=out_shape,
            in_specs=specs + [IN_ANY] * len(after),
            out_specs=outs,
            cost_estimate=pl.CostEstimate(
                flops=int(micros * FLOPS_IN_MICRO), bytes_accessed=0, transcendentals=0
            ),
            compiler_params=pltpu.CompilerParams(vmem_limit_bytes=limit * MIB),
        )(*args, *after)

    return run


def tie(values, after):
    count = len(values)

    def nothing(*refs):
        pass

    return pl.pallas_call(
        nothing,
        out_shape=[jax.ShapeDtypeStruct(v.shape, v.dtype) for v in values],
        in_specs=[IN_ANY] * (count + len(after)),
        out_specs=[IN_ANY] * count,
        input_output_aliases={i: i for i in range(count)},
        compiler_params=pltpu.CompilerParams(vmem_limit_bytes=MIB),
    )(*values, *after)


def shape(*dims):
    return jax.ShapeDtypeStruct(dims, BF16)


FLAG = shape(16, 128)
FLOPS_IN_MICRO = 1.15e7


def shift(block, step, second):
    pairs = []
    for core in range(2):
        for y in range(SIDE):
            for x in range(SIDE):
                if (core == 0) != second:
                    target = y * SIDE + (x + step) % SIDE
                else:
                    target = (y + step) % SIDE * SIDE + x
                base = core * SIDE * SIDE
                pairs.append((base + y * SIDE + x, base + target))
    return lax.ppermute(block, ("dp", "tensor"), pairs)


def swap(block):
    return lax.ppermute(block, "dp", [(0, 1), (1, 0)])


def exchange(rows, parts):
    blocks = rows.reshape(parts, rows.shape[0] // parts, rows.shape[1])
    moved = lax.all_to_all(blocks, ("dp", "expert"), split_axis=0, concat_axis=0, tiled=True)
    return moved.reshape(rows.shape)


def spread(ids, gates, experts):
    tokens = ids.shape[1]
    dims = (experts * 2 * SLOTS, tokens)
    row = lax.broadcasted_iota(jnp.int32, dims, 0)
    expert, half, slot = row // (2 * SLOTS), row // SLOTS % 2, row % SLOTS
    first, second = ids[0:1, :] == expert, ids[1:2, :] == expert
    named = jnp.where(first | second, 1.0, 0.0).astype(F32)
    earlier = lax.broadcasted_iota(jnp.int32, (tokens, tokens), 0)
    later = lax.broadcasted_iota(jnp.int32, (tokens, tokens), 1)
    place = dot(named, jnp.where(earlier < later, 1.0, 0.0).astype(F32))
    select = jnp.where(place == slot.astype(F32), named, 0.0)
    weight = jnp.where(first, gates[0:1, :], 0.0) + jnp.where(second, gates[1:2, :], 0.0)
    weighted = select * weight
    return (
        [jnp.where(half == h, select, 0.0) for h in range(2)],
        [jnp.where(half == h, weighted, 0.0) for h in range(2)],
    )


def dispatch_kernel(experts, ids_ref, gates_ref, tokens_ref, cotangent_ref, opened, send_ref):
    select, weighted = spread(ids_ref[...], gates_ref[...].astype(F32), experts)
    width = tokens_ref.shape[1] // 2
    rows = experts * 2 * SLOTS
    for mats, ref, start in ((select, tokens_ref, 0), (weighted, cotangent_ref, rows)):
        low, high = (mat.astype(BF16) for mat in mats)
        total = dot(low, ref[:, :width]) + dot(high, ref[:, width:])
        send_ref[start : start + rows, :] = total.astype(BF16)


def open_kernel(flag):
    flag[...] = jnp.zeros_like(flag)


def dispatch(experts, *args):
    rows = 4 * experts * SLOTS
    opened = call(open_kernel, FLAG, micros=1500)()
    return pl.pallas_call(
        functools.partial(dispatch_kernel, experts),
        out_shape=shape(rows, args[2].shape[1] // 2),
        in_specs=[IN_VMEM] * 4 + [IN_ANY],
        out_specs=IN_VMEM,
        compiler_params=pltpu.CompilerParams(vmem_limit_bytes=16 * MIB),
    )(*args, opened)


def combine_kernel(experts, ids_ref, gates_ref, home_ref, out_ref, back_ref):
    select, weighted = spread(ids_ref[...], gates_ref[...].astype(F32), experts)
    width = out_ref.shape[1] // 2
    rows = experts * 2 * SLOTS
    for mats, ref, start in ((weighted, out_ref, 0), (select, back_ref, rows)):
        part = home_ref[start : start + rows, :]
        for h in range(2):
            mat = mats[h].astype(BF16)
            ref[:, h * width : (h + 1) * width] = dot(mat, part, 0, 0).astype(BF16)


def half_matrix(rows, half, flip):
    dims = (2 * rows, rows) if flip else (rows, 2 * rows)
    plain = lax.broadcasted_iota(jnp.int32, dims, 1 if flip else 0)
    mixed = lax.broadcasted_iota(jnp.int32, dims, 0 if flip else 1)
    same = (mixed // (2 * SLOTS) == plain // SLOTS) & (mixed % SLOTS == plain % SLOTS)
    return jnp.where(same & (mixed // SLOTS % 2 == half), 1.0, 0.0).astype(BF16)


def unmix_kernel(mixed_ref, rows_ref):
    width = mixed_ref.shape[1]
    mixed = mixed_ref[...]
    for h in range(2):
        part = dot(half_matrix(rows_ref.shape[0], h, False), mixed)
        rows_ref[:, h * width : (h + 1) * width] = part.astype(BF16)


def load_kernel(*refs):
    for source, target in zip(refs[:3], refs[3:6]):
        target[...] = source[...]
    refs[6][...] = jnp.zeros_like(refs[6])


def join_kernel(top_ref, bottom_ref, rows_ref):
    rows = top_ref.shape[0]
    rows_ref[:rows, :] = top_ref[...]
    rows_ref[rows:, :] = bottom_ref[...]


def first_kernel(*refs):
    *pieces, gate_own, gate_far, up_own, up_far, down_own, down_far, act_ref = refs
    units = gate_own.shape[1]
    rows = pieces[0].shape[0]

    @pl.when(lax.axis_index("dp") == 0)
    def _():
        for i in range(0, len(pieces), 2):
            x = jnp.concatenate([p[...] for p in pieces[i : i + 2]], axis=0)
            at = slice(i * rows, (i + 2) * rows)
            for j, (gate, up) in enumerate(((gate_own, up_own), (gate_far, up_far))):
                gate_proj = dot(x, gate[...])
                up_proj = dot(x, up[...])
                sig = jax.nn.sigmoid(gate_proj)
                active = gate_proj * sig
                slope = up_proj * sig * (1.0 + gate_proj * (1.0 - sig))
                for k, value in enumerate((slope, active, active * up_proj)):
                    start = (2 * k + j) * units
                    act_ref[at, start : start + units] = value.astype(BF16)

    @pl.when(lax.axis_index("dp") != 0)
    def _():
        for i in range(0, len(pieces), 2):
            dy = jnp.concatenate([p[...] for p in pieces[i : i + 2]], axis=0)
            at = slice(i * rows, (i + 2) * rows)
            for j, down in enumerate((down_far, down_own)):
                value = dot(dy, down[...], 1, 1).astype(BF16)
                for k in range(2):
                    start = (2 * k + j) * units
                    act_ref[at, start : start + units] = value
                start = (4 + j) * units
                act_ref[at, start : start + units] = jnp.ones_like(value)


def block_of(refs, line, inner, rows):
    ref = refs[(0, 1, 1, 2)[line]]
    start = ((0, 0, 1, 0)[line] * SIDE + inner) * rows
    return ref[start : start + rows, :]


def line_product(mine, far, line, rows):
    return jnp.concatenate(
        [
            block_of(mine, line, inner, rows) * block_of(far, inner, line, rows)
            for inner in range(SIDE)
        ],
        axis=0,
    )


def second(product, weights, stores):
    gate_own, gate_far, up_own, up_far, down_own, down_far = weights
    units = gate_own.shape[1]
    width = down_own.shape[1]
    step = 512
    starts = [0]
    for ref in stores:
        starts.append(starts[-1] + ref.shape[0])

    @pl.when(lax.axis_index("dp") == 0)
    def _():
        for c in range(0, width, step):
            total = dot(product[:, 4 * units : 5 * units], down_own[:, c : c + step]) + dot(
                product[:, 5 * units :], down_far[:, c : c + step]
            )
            for i, ref in enumerate(stores):
                ref[:, c : c + step] = total[starts[i] : starts[i + 1]].astype(BF16)

    @pl.when(lax.axis_index("dp") != 0)
    def _():
        for c in range(0, width, step):
            total = dot(product[:, :units], gate_far[c : c + step, :], 1, 1)
            for k, ref in enumerate((gate_own, up_far, up_own)):
                part = product[:, (k + 1) * units : (k + 2) * units]
                total = total + dot(part, ref[c : c + step, :], 1, 1)
            for i, ref in enumerate(stores):
                ref[:, c : c + step] = total[starts[i] : starts[i + 1]].astype(BF16)


def far_early_kernel(rows, mine, own_far, side_far, *refs):
    weights, low_store, two_store = refs[:6], refs[6], refs[7]
    far = (own_far, side_far)
    product = jnp.concatenate(
        [mine[i * rows : (i + 1) * rows, :] * block_of(far, i, 3, rows) for i in range(3)], axis=0
    )
    second(product, weights, (low_store, two_store))


def far_last_kernel(rows, mine, far, *refs):
    weights, store, flag = refs[:6], refs[6], refs[7]
    flag[...] = jnp.zeros_like(flag)
    second(mine[3 * rows :, :] * far[3 * rows :, :], weights, (store,))


def lines_kernel(rows, lines, *refs):
    mine, far, weights, stores, flag = refs[:3], refs[3:6], refs[6:12], refs[12:-1], refs[-1]
    flag[...] = jnp.zeros_like(flag)
    for i, line in enumerate(lines):
        product = line_product(mine, far, line, rows)
        second(product, weights, stores[2 * i : 2 * i + 2])


def own_line_kernel(rows, *refs):
    mine, far, weights, stores, act = refs[:3], refs[3:6], refs[6:12], refs[12:14], refs[14]
    for line in range(SIDE):
        product = line_product(mine, far, line, rows)
        act[line * SIDE * rows : (line + 1) * SIDE * rows, :] = product
        if line == 0:
            second(product, weights, stores)


STEP = 256


def column(pieces, at):
    return jnp.concatenate([p[:, at] for p in pieces], axis=0)


def columns_loop(width, body):
    def one(i, carry):
        body(pl.ds(pl.multiple_of(i * STEP, STEP), STEP))
        return carry

    lax.fori_loop(0, width // STEP, one, 0)


def far_grads_kernel(*refs):
    *pieces, act, send, send_more, flag = refs
    units = send.shape[1]
    flag[...] = jnp.zeros_like(flag)

    @pl.when(lax.axis_index("dp") == 0)
    def _():
        factor = jnp.concatenate(
            [act[:, units : 2 * units], act[:, 3 * units : 4 * units]], axis=1
        )

        def one(at):
            total = dot(column(pieces, at), factor, 0, 0).astype(BF16)
            send[at, :] = total[:, :units]
            send_more[at, :] = total[:, units:]

        columns_loop(send.shape[0], one)

    @pl.when(lax.axis_index("dp") != 0)
    def _():
        hidden = act[:, 4 * units : 5 * units].T

        def one(at):
            send[at, :] = dot(hidden, column(pieces, at)).astype(BF16)

        columns_loop(send.shape[0], one)


def own_grads_kernel(*refs):
    *pieces, act, got, got_more, gate_ref, up_ref, down_ref, flag = refs
    flag[...] = jnp.zeros_like(flag)
    units = gate_ref.shape[1]
    width = gate_ref.shape[0]

    @pl.when(lax.axis_index("dp") == 0)
    def _():
        factor = jnp.concatenate([act[:, :units], act[:, 2 * units : 3 * units]], axis=1)

        def one(at):
            total = dot(column(pieces, at), factor, 0, 0).astype(BF16)
            gate_ref[at, :] = total[:, :units]
            up_ref[at, :] = total[:, units:]
            down_ref[:, at] = got[at, :]

        columns_loop(width, one)

    @pl.when(lax.axis_index("dp") != 0)
    def _():
        hidden = act[:, 5 * units :].T

        def one(at):
            down_ref[:, at] = dot(hidden, column(pieces, at)).astype(BF16)
            gate_ref[at, :] = got[at, :]
            up_ref[at, :] = got_more[at, :]

        columns_loop(width, one)


def add(*parts):
    total = parts[0].astype(F32)
    for part in parts[1:]:
        total = total + part.astype(F32)
    return total.astype(BF16)


def relay_sum_kernel(own, *refs):
    got, total, flag = refs[:-2], refs[-2], refs[-1]
    rows = got[0].shape[0]
    for i, ref in enumerate(got):
        at = slice(i * rows, (i + 1) * rows)
        total[at, :] = add(own[at, :], ref[...])
    flag[...] = jnp.zeros_like(flag)


def line_sum_kernel(*refs):
    low, high, outs, flag = refs[:3], refs[3:6], refs[6:10], refs[10]
    flag[...] = jnp.zeros_like(flag)
    rows = outs[0].shape[0]
    for i, group in enumerate((low, high)):
        for j in range(2):
            at = slice(j * rows, (j + 1) * rows)
            outs[2 * i + j][...] = add(*[r[at, :] for r in group])


def home_kernel(own, one, two, three, mixed_ref):
    rows, width = own.shape
    total = add(own[...], one[...], two[...], three[...])
    low = dot(half_matrix(rows, 0, True), total[:, : width // 2])
    high = dot(half_matrix(rows, 1, True), total[:, width // 2 :])
    mixed_ref[...] = (low + high).astype(BF16)


def body(tokens, expert_ids, gate_values, cotangent, w_gate, w_up, w_down):
    tok_rows, width = tokens.shape
    experts = lax.axis_size("expert")
    sources = 2 * experts
    rows = sources * SLOTS
    units = w_gate.shape[2]
    ids, gates = expert_ids.T, gate_values.T

    shards = (w_gate[0], w_up[0], w_down[0])
    others = [swap(w) for w in shards]

    rows_out = dispatch(experts, ids, gates, tokens, cotangent)
    mixed = exchange(rows_out, sources)
    mine = call(unmix_kernel, shape(rows, width), after=others)(mixed)

    plus = shift(mine, -1, False)
    minus = shift(mine, 1, False)
    far = shift(mine, 2, False)
    *owns, loaded = call(
        load_kernel, tuple(shape(*w.shape) for w in shards) + (FLAG,), after=(mine,)
    )(*shards)
    weights = [w for pair in zip(owns, others) for w in pair]
    low = call(join_kernel, shape(2 * rows, width), after=(loaded,))(mine, plus)
    high = call(join_kernel, shape(2 * rows, width))(minus, far)
    low_minus = shift(low, 1, True)
    high_plus = shift(high, -1, True)
    high_minus = shift(high, 1, True)
    low_plus = shift(low, -1, True)

    def first(*pieces, micros=2):
        count = len(pieces) * pieces[0].shape[0]
        return call(
            first_kernel, shape(count, 6 * units), micros=micros, limit=18
        )(*pieces, *weights)

    act_own = first(low, high)
    (low_minus,) = tie((low_minus,), (act_own,))
    low_far = shift(low_minus, 1, True)
    high_far = shift(high_plus, -1, True)
    line = SIDE * rows
    acts = [
        act_own,
        first(low_plus, high_plus, low_minus, high_minus),
        first(low_far, high_far, micros=1000),
    ]
    far_acts = [swap(a) for a in acts]
    pieces = (low, high, low_plus, high_plus, low_minus, high_minus, low_far, high_far)

    half = shape(line // 2, width)

    block = shape(rows, width)
    out_low_far, out_far_two = call(
        functools.partial(far_early_kernel, rows), (half, block), limit=18
    )(acts[2], far_acts[0], far_acts[1], *weights)
    low_got = shift(out_low_far, -1, True)
    two_got = shift(out_far_two, 1, True)
    out_far_three, last = call(
        functools.partial(far_last_kernel, rows), (block, FLAG), limit=18
    )(acts[2], far_acts[2], *weights)
    three_got = shift(out_far_three, 1, True)
    def lines(*which):
        return call(
            functools.partial(lines_kernel, rows, which),
            (half,) * (2 * len(which)) + (FLAG,),
            micros=1.5 * len(which),
            limit=18,
            after=(last,),
        )(*acts, *far_acts, *weights)

    out_low_plus, out_high_plus, out_low_minus, out_high_minus, sides = lines(1, 2)
    high_one = shift(out_high_minus, -1, True)
    low_one = shift(out_low_plus, 1, True)
    relay_sum = call(relay_sum_kernel, (half, FLAG))
    low_sum, low_relayed = relay_sum(out_low_minus, low_got)
    low_two = shift(low_sum, -1, True)
    high_sum, high_relayed = relay_sum(out_high_plus, two_got, three_got)
    high_two = shift(high_sum, 1, True)
    out_low, out_high, act = call(
        functools.partial(own_line_kernel, rows),
        (half, half, shape(SIDE * line, 6 * units)),
        micros=1.5,
        limit=18,
        after=(sides,),
    )(*acts, *far_acts, *weights)

    column_shape, flat_shape = shape(width, units), shape(units, width)
    send, send_more, sent = call(
        far_grads_kernel,
        (column_shape, column_shape, FLAG),
        micros=8,
        limit=18,
        after=(low_relayed, high_relayed),
    )(*pieces, act)
    got, got_more = swap(send), swap(send_more)

    block = shape(rows, width)
    own, plus_sum, minus_sum, far_sum, summed = call(
        line_sum_kernel, (block,) * 4 + (FLAG,), micros=1500, after=(sent,)
    )(out_low, low_one, low_two, out_high, high_one, high_two)
    got_plus = shift(plus_sum, 1, False)
    got_minus = shift(minus_sum, -1, False)
    got_far = shift(far_sum, 2, False)
    d_gate, d_up, d_down, settled = call(
        own_grads_kernel,
        (column_shape, column_shape, flat_shape, FLAG),
        micros=8,
        limit=18,
        after=(summed,),
    )(*pieces, act, got, got_more)
    back = call(home_kernel, shape(2 * rows, width // 2), after=(settled,))(
        own, got_plus, got_minus, got_far
    )
    home = exchange(back, sources)

    token_shape = shape(tok_rows, width)
    moe_out, d_tokens = call(
        functools.partial(combine_kernel, experts), (token_shape, token_shape)
    )(ids, gates, home)
    return moe_out, d_tokens, d_gate[None], d_up[None], d_down[None]


def solution(mesh):
    token_spec = P(("dp", "expert", "tensor"), None)
    column_spec = P("expert", None, ("dp", "tensor"))
    row_spec = P("expert", ("dp", "tensor"), None)
    in_specs = (token_spec,) * 4 + (column_spec, column_spec, row_spec)
    out_specs = (token_spec, token_spec, column_spec, column_spec, row_spec)
    return jax.shard_map(body, mesh=mesh, in_specs=in_specs, out_specs=out_specs, check_vma=False)
```
